128 devices in a mesh: row: 8 (over x, core), col: 16 (over z, y).
Axes of the slice: x: 4, y: 4, z: 4, core: 2. Of those that a mesh axis runs over, the one named last changes fastest.
Arguments:
- features: bfloat16 [128, 512, 192], P('row', 'col'), may hold values from -6 to 6
- selectors: bfloat16 [128, 512, 4, 16], P('row', 'col'), may hold values from -2 to 2
- log_decay: bfloat16 [128, 512, 2, 6], P('row', 'col'), may hold values from -0.8 to 0, as said below
- in_weight: bfloat16 [192, 768], replicated, may hold values from -0.4375 to 0.4375
- out_weight: bfloat16 [384, 192], replicated, may hold values from -0.3125 to 0.3125
- cotangent: bfloat16 [128, 512, 192], P('row', 'col'), may hold values from -6 to 6
Outputs:
- block_out: bfloat16 [128, 512, 192], P('row', 'col')
- input_grad: bfloat16 [128, 512, 192], P('row', 'col')
- in_weight_grad: float32 [192, 768], replicated
- out_weight_grad: float32 [384, 192], replicated
The draws below stay inside these ranges and needn't reach their ends.
Inputs may be any that keep to these rules, and one draw needn't show every extreme that they name: `log_decay`: log-decays are negative.
All inputs are finite; a program needn't handle non-finite values.
Results may differ from the reference program's by a relative error of at most 0.012.
Values may be sent and summed in bfloat16 or wider, within the bound.
No kernel may reach another device: no remote copies, remote signals or barrier semaphores. Data moves between devices by JAX's collectives and lax.ppermute only.
A program may use at most 128 MiB of HBM per device.

```python
import jax
import jax.numpy as jnp
from jax import lax

D = 192
E = 384
STATE = 16
HEAD_TOTAL = 6
ROWS_DEV = 16
COLS_DEV = 32
MAP_TOKEN_ROWS = 128
MAP_TOKEN_COLUMNS = 512
TOKENS = 65536


def draw_log_decay(key, part):
    random_keys = jax.random.split(key, 7)
    head_shape = (1, 1, 2, HEAD_TOTAL)
    fast_share = 0.5
    fast_heads = jax.random.uniform(random_keys[0], head_shape) < fast_share
    position_index = jnp.arange(2).reshape(1, 1, 2, 1)
    chain_len = jnp.where(position_index == 0, jnp.float32(MAP_TOKEN_COLUMNS), jnp.float32(MAP_TOKEN_ROWS))
    slow_rate = jax.random.uniform(random_keys[1], head_shape, minval=0.1, maxval=1.5) / chain_len
    fast_rate = jax.random.uniform(random_keys[2], head_shape, minval=1.0 / 50.0, maxval=1.0 / 30.0)
    default_decay_rate = jnp.where(fast_heads, fast_rate, slow_rate)
    random_offset = jnp.exp(jax.random.uniform(random_keys[3], (MAP_TOKEN_ROWS, MAP_TOKEN_COLUMNS, 2, HEAD_TOTAL), minval=-0.693, maxval=0.693))
    across_columns = jax.random.uniform(random_keys[4], (1, MAP_TOKEN_COLUMNS, 1, HEAD_TOTAL)) < 2.0 / MAP_TOKEN_COLUMNS
    across_rows = jax.random.uniform(random_keys[5], (MAP_TOKEN_ROWS, 1, 1, HEAD_TOTAL)) < 2.0 / MAP_TOKEN_ROWS
    decay_groups = jnp.where(position_index == 0, across_columns, across_rows)
    group_depth = jax.random.uniform(random_keys[6], (MAP_TOKEN_ROWS, MAP_TOKEN_COLUMNS, 2, HEAD_TOTAL), minval=0.22, maxval=0.69)
    sampled = -(default_decay_rate * random_offset + jnp.where(decay_groups, group_depth, 0.0))
    return sampled.astype(jnp.float32).astype(jnp.bfloat16)


def block_levels(stream_key, extent, cuts, smallest, high):
    loudness, own = 1.0, jax.random.fold_in(stream_key, 6)
    for dim, shards_of in cuts:
        draws = jnp.exp(jax.random.uniform(jax.random.fold_in(own, dim), (shards_of,), jnp.float32, smallest / len(cuts), high / len(cuts)))
        loudness = loudness * jnp.repeat(draws, extent[dim] // shards_of).reshape([-1 if axis == dim else 1 for axis in range(len(extent))])
    return loudness


def noise(rng, shape, width, bound, cuts=(), dtype=jnp.bfloat16):
    result = jax.random.normal(rng, shape, jnp.float32) * width
    if len(cuts) > 0:
        result = block_levels(rng, shape, cuts, -0.22, 0.18) * result
    return jnp.clip(result, min=-bound, max=bound).astype(dtype)


def setup_inputs(seed: int = 0) -> dict:
    splits = jax.random.split(jax.random.key(seed), 7)
    features = noise(splits[0], (MAP_TOKEN_ROWS, MAP_TOKEN_COLUMNS, D), 1.0, 6.0, ((0, 8), (1, 16)))
    selectors = noise(splits[1], (MAP_TOKEN_ROWS, MAP_TOKEN_COLUMNS, 4, STATE), (0.5 * (MAP_TOKEN_ROWS * MAP_TOKEN_COLUMNS) ** -0.125), 2.0, ((0, 8), (1, 16)))
    log_decay = draw_log_decay(jax.random.fold_in(splits[6], 71), 0)
    in_weight = noise(splits[3], (D, 2 * E), D ** -0.5, 0.4375)
    out_weight = noise(splits[4], (E, D), E ** -0.5, 0.3125)
    cotangent = noise(splits[5], (MAP_TOKEN_ROWS, MAP_TOKEN_COLUMNS, D), 1.0, 6.0, ((0, 8), (1, 16)))
    return dict(features=features, selectors=selectors, log_decay=log_decay, in_weight=in_weight, out_weight=out_weight, cotangent=cotangent)


HIGHEST_PRECISION = lax.Precision.HIGHEST


def forward_local(values, b_sel, c_sel, log_step):
    batch_size, length, channels = values.shape
    head_count = log_step.shape[2]
    head_dim = channels // head_count
    cumlog = jnp.cumsum(log_step.astype(jnp.float32), axis=1)
    totals = cumlog[:, -1]
    scores = jnp.einsum("btn,bsn->bts", c_sel, b_sel, preferred_element_type=jnp.float32)
    positions = jnp.arange(length)
    causal = positions[:, None] >= positions[None, :]
    spread = cumlog[:, :, None, :] - cumlog[:, None, :, :]
    weights = jnp.exp(jnp.where(causal[None, :, :, None], spread, -jnp.inf)) * scores[:, :, :, None]
    per_head = values.astype(jnp.float32).reshape(batch_size, length, head_count, head_dim)
    output = jnp.einsum("btsh,bshp->bthp", weights, per_head, precision=HIGHEST_PRECISION)
    fading = jnp.exp(totals[:, None, :] - cumlog)
    states = jnp.einsum("bsh,bshp,bsn->bhpn", fading, per_head, b_sel.astype(jnp.float32), precision=HIGHEST_PRECISION)
    return output.reshape(batch_size, length, channels), totals, states, cumlog


def add_incoming(output, c_sel, cumlog, incoming):
    batch_size, length, channels = output.shape
    carried_term = jnp.exp(cumlog)[:, :, :, None] * jnp.einsum("bhpn,btn->bthp", incoming, c_sel.astype(jnp.float32), precision=HIGHEST_PRECISION)
    return output + carried_term.reshape(batch_size, length, channels)


def backward_local(adjoint, b_sel, c_sel, log_step):
    batch_size, length, channels = adjoint.shape
    head_count = log_step.shape[2]
    head_dim = channels // head_count
    cumlog = jnp.cumsum(log_step.astype(jnp.float32), axis=1)
    totals = cumlog[:, -1]
    scores = jnp.einsum("bsn,btn->bst", b_sel, c_sel, preferred_element_type=jnp.float32)
    positions = jnp.arange(length)
    onward = positions[:, None] <= positions[None, :]
    spread = cumlog[:, None, :, :] - cumlog[:, :, None, :]
    weights = jnp.exp(jnp.where(onward[None, :, :, None], spread, -jnp.inf)) * scores[:, :, :, None]
    per_head = adjoint.astype(jnp.float32).reshape(batch_size, length, head_count, head_dim)
    output = jnp.einsum("bsth,bthp->bshp", weights, per_head, precision=HIGHEST_PRECISION)
    rising = jnp.exp(cumlog)
    states = jnp.einsum("bth,bthp,btn->bhpn", rising, per_head, c_sel.astype(jnp.float32), precision=HIGHEST_PRECISION)
    return output.reshape(batch_size, length, channels), totals, states, cumlog


def add_outgoing(output, b_sel, cumlog, totals, incoming):
    batch_size, length, channels = output.shape
    carried_term = jnp.exp(totals[:, None, :] - cumlog)[:, :, :, None] * jnp.einsum("bhpn,bsn->bshp", incoming, b_sel.astype(jnp.float32), precision=HIGHEST_PRECISION)
    return output + carried_term.reshape(batch_size, length, channels)


def blocked(array, block_len):
    dims_in = array.shape
    return jnp.swapaxes(array.reshape((dims_in[0], dims_in[1] // block_len, block_len) + dims_in[2:]), 0, 1)


def unblock(array):
    swapped = jnp.swapaxes(array, 0, 1)
    dims_in = swapped.shape
    return swapped.reshape((dims_in[0], dims_in[1] * dims_in[2]) + dims_in[3:])


def run_forward(values, b_sel, c_sel, log_step, block_len):
    batch_size, length, channels = values.shape
    head_count = log_step.shape[2]
    initial = jnp.zeros((batch_size, head_count, channels // head_count, b_sel.shape[2]), jnp.float32)

    def advance(carried, pieces):
        output, totals, states, cumlog = forward_local(pieces[0], pieces[1], pieces[2], pieces[3])
        output = add_incoming(output, pieces[2], cumlog, carried)
        return jnp.exp(totals)[:, :, None, None] * carried + states, output

    stacked = (blocked(values, block_len), blocked(b_sel, block_len), blocked(c_sel, block_len), blocked(log_step, block_len))
    _, outputs = lax.scan(advance, initial, stacked)
    return unblock(outputs)


def run_backward(adjoint, b_sel, c_sel, log_step, block_len):
    batch_size, length, channels = adjoint.shape
    head_count = log_step.shape[2]
    initial = jnp.zeros((batch_size, head_count, channels // head_count, b_sel.shape[2]), jnp.float32)

    def advance(carried, pieces):
        output, totals, states, cumlog = backward_local(pieces[0], pieces[1], pieces[2], pieces[3])
        output = add_outgoing(output, pieces[1], cumlog, totals, carried)
        return jnp.exp(totals)[:, :, None, None] * carried + states, output

    stacked = (blocked(adjoint, block_len), blocked(b_sel, block_len), blocked(c_sel, block_len), blocked(log_step, block_len))
    _, outputs = lax.scan(advance, initial, stacked, reverse=True)
    return unblock(outputs)


def reference(features, selectors, log_decay, in_weight, out_weight, cotangent):
    row_groups = MAP_TOKEN_ROWS // ROWS_DEV
    col_groups = MAP_TOKEN_COLUMNS // COLS_DEV

    def section_rows(grouped):
        feature_block, selector_block, decay_block = grouped
        projected = jnp.dot(feature_block.reshape(-1, D), in_weight, preferred_element_type=jnp.float32)
        scan_values = projected[:, :E].astype(jnp.bfloat16).reshape(ROWS_DEV, MAP_TOKEN_COLUMNS, E)
        gates = projected[:, E:].astype(jnp.bfloat16).reshape(ROWS_DEV, MAP_TOKEN_COLUMNS, E)
        row_out = run_forward(scan_values, selector_block[:, :, 0], selector_block[:, :, 1], decay_block[:, :, 0], COLS_DEV).astype(jnp.bfloat16)
        return row_out, gates

    row_out, gates = lax.map(section_rows, (features.reshape(row_groups, ROWS_DEV, MAP_TOKEN_COLUMNS, D), selectors.reshape(row_groups, ROWS_DEV, MAP_TOKEN_COLUMNS, 4, STATE), log_decay.reshape(row_groups, ROWS_DEV, MAP_TOKEN_COLUMNS, 2, HEAD_TOTAL)))
    row_out = row_out.reshape(MAP_TOKEN_ROWS, MAP_TOKEN_COLUMNS, E)
    gates = gates.reshape(MAP_TOKEN_ROWS, MAP_TOKEN_COLUMNS, E)

    def by_columns(array):
        swapped = jnp.swapaxes(array, 0, 1)
        return swapped.reshape((col_groups, COLS_DEV) + swapped.shape[1:])

    def section_cols(grouped):
        row_block, gate_block, selector_block, decay_block, feature_block, cot_block = grouped
        col_out = run_forward(row_block, selector_block[:, :, 2], selector_block[:, :, 3], decay_block[:, :, 1], ROWS_DEV).astype(jnp.bfloat16)
        col_float = col_out.astype(jnp.float32)
        gate_float = gate_block.astype(jnp.float32)
        sigmoid_gate = jax.nn.sigmoid(gate_float)
        hidden = (col_float * gate_float * sigmoid_gate).astype(jnp.bfloat16)
        mixed = jnp.dot(hidden.reshape(-1, E), out_weight, preferred_element_type=jnp.float32).reshape(COLS_DEV, MAP_TOKEN_ROWS, D)
        block_out = (feature_block.astype(jnp.float32) + mixed).astype(jnp.bfloat16)
        hidden_grad = jnp.dot(cot_block.reshape(-1, D), out_weight.T, preferred_element_type=jnp.float32).reshape(COLS_DEV, MAP_TOKEN_ROWS, E)
        col_grad = (hidden_grad * gate_float * sigmoid_gate).astype(jnp.bfloat16)
        gate_grad = (hidden_grad * col_float * sigmoid_gate * (1.0 + gate_float * (1.0 - sigmoid_gate))).astype(jnp.bfloat16)
        row_grad = run_backward(col_grad, selector_block[:, :, 2], selector_block[:, :, 3], decay_block[:, :, 1], ROWS_DEV).astype(jnp.bfloat16)
        out_part = jnp.dot(hidden.reshape(-1, E).T, cot_block.reshape(-1, D), preferred_element_type=jnp.float32)
        return block_out, gate_grad, row_grad, out_part

    col_results = lax.map(section_cols, (by_columns(row_out), by_columns(gates), by_columns(selectors), by_columns(log_decay), by_columns(features), by_columns(cotangent)))

    def by_rows(array):
        merged = array.reshape((MAP_TOKEN_COLUMNS,) + array.shape[2:])
        return jnp.swapaxes(merged, 0, 1)

    block_out = by_rows(col_results[0])
    gate_grad = by_rows(col_results[1])
    row_grad = by_rows(col_results[2])
    out_total = jnp.sum(col_results[3], axis=0)

    def section_back(grouped):
        grad_block, gate_block, selector_block, decay_block, feature_block, cot_block = grouped
        value_grad = run_backward(grad_block, selector_block[:, :, 0], selector_block[:, :, 1], decay_block[:, :, 0], COLS_DEV).astype(jnp.bfloat16)
        joined = jnp.concatenate([value_grad, gate_block], axis=-1).reshape(-1, 2 * E)
        pulled = jnp.dot(joined, in_weight.T, preferred_element_type=jnp.float32).reshape(ROWS_DEV, MAP_TOKEN_COLUMNS, D)
        input_grad = (cot_block.astype(jnp.float32) + pulled).astype(jnp.bfloat16)
        in_part = jnp.dot(feature_block.reshape(-1, D).T, joined, preferred_element_type=jnp.float32)
        return input_grad, in_part

    back_results = lax.map(section_back, (row_grad.reshape(row_groups, ROWS_DEV, MAP_TOKEN_COLUMNS, E), gate_grad.reshape(row_groups, ROWS_DEV, MAP_TOKEN_COLUMNS, E), selectors.reshape(row_groups, ROWS_DEV, MAP_TOKEN_COLUMNS, 4, STATE), log_decay.reshape(row_groups, ROWS_DEV, MAP_TOKEN_COLUMNS, 2, HEAD_TOTAL), features.reshape(row_groups, ROWS_DEV, MAP_TOKEN_COLUMNS, D), cotangent.reshape(row_groups, ROWS_DEV, MAP_TOKEN_COLUMNS, D)))
    input_grad = back_results[0].reshape(MAP_TOKEN_ROWS, MAP_TOKEN_COLUMNS, D)
    in_total = jnp.sum(back_results[1], axis=0)
    scale = jnp.float32(TOKENS) ** -0.5
    return block_out, input_grad, in_total * scale, out_total * scale
```

```python
import jax
import jax.numpy as jnp
from jax import lax
from jax.experimental import pallas as pl
from jax.experimental.pallas import tpu as pltpu
from jax.sharding import PartitionSpec as P

BF = jnp.bfloat16
F32 = jnp.float32
MODEL = 192
CHAN = 384
TOK = 512
GROUP = 256
VMEM_LIMIT = 48 * 1024 * 1024


def iota(shape, dim):
    return lax.broadcasted_iota(jnp.int32, shape, dim)


def mm(a, b):
    return jnp.dot(a, b, preferred_element_type=F32)


def mm_t(a, b):
    return lax.dot_general(a, b, (((1,), (1,)), ((), ())), preferred_element_type=F32)


def t_mm(a, b):
    return lax.dot_general(a, b, (((0,), (0,)), ((), ())), preferred_element_type=F32)


def spread(aux, first):
    pick = (iota((256, 128), 0) - first == iota((256, 128), 1) % 16).astype(F32).astype(BF)
    return mm(aux, pick)


def scan_tokens(aux, values, by_row, forward):
    token = iota((TOK, 128), 0)
    chunk = token // 64 if by_row else (token // GROUP) * 4 + token % 4
    member = (iota((TOK, 128), 1) // 16 == chunk).astype(F32)
    b_part = (spread(aux, 192) * member).astype(BF)
    c_part = (spread(aux, 208) * member).astype(BF)
    heads = (iota((256, CHAN), 0) - 224 == iota((256, CHAN), 1) // 64).astype(F32).astype(BF)
    log_step = mm(aux, heads).astype(BF)
    here, there = iota((GROUP, GROUP), 0), iota((GROUP, GROUP), 1)
    same = (here // 64 == there // 64) if by_row else (here % 4 == there % 4)
    if forward:
        order, counted, src, out = there <= here, there <= here, b_part, c_part
    else:
        order, counted, src, out = there >= here, there > here, c_part, b_part
    add_up = (same & counted).astype(F32).astype(BF)
    halves = [slice(0, GROUP), slice(GROUP, TOK)]
    run = [mm(add_up, log_step[h]) for h in halves]
    raised = [(jnp.exp(-run[i]) * values[h]).astype(BF) for i, h in enumerate(halves)]
    states = t_mm(src[halves[0]], raised[0]) + t_mm(src[halves[1]], raised[1])
    decay = jnp.exp(t_mm(member.astype(BF), log_step))
    zero = jnp.zeros((16, CHAN), F32)
    carried = [zero] * 8
    part = lambda array, k: array[16 * k : 16 * k + 16]
    if by_row:
        steps = [(k, k + 1) for k in range(7)] if forward else [(k, k - 1) for k in range(7, 0, -1)]
    else:
        steps = [(j, j + 4) for j in range(4)] if forward else [(j + 4, j) for j in range(4)]
    for old, new in steps:
        carried[new] = part(decay, old) * (carried[old] + part(states, old))
    coming = jnp.concatenate(carried, axis=0).astype(BF)
    result = []
    for i, h in enumerate(halves):
        scores = jnp.where(order, mm_t(out[h], src[h]), 0.0).astype(BF)
        result.append(jnp.exp(run[i]) * (mm(scores, raised[i]) + mm(out[h], coming)))
    return jnp.concatenate(result, axis=0)


def to_columns(scratch, slot, token_rows):
    for l in range(CHAN // 128):
        for r in range(8):
            for j in range(4):
                scratch[l, pl.ds(r * 128 + slot + j, 16, stride=8), :] = token_rows[
                    l, pl.ds(4 * r + j, 16, stride=32), :
                ]


def split_lanes(ref, value):
    for l in range(value.shape[1] // 128):
        ref[l] = value[:, 128 * l : 128 * l + 128]


def send_rows_kernel(place, packed, cot, *outs):
    x, core = place[0] // 2, place[0] % 2
    slot = iota((TOK, 1), 0)
    q, row, j = slot // 64, (slot % 64) // 4, slot % 4
    dest = ((x + q // 2) % 4) * 2 + (core + q % 2) % 2
    pick = ((row * 32 + 4 * dest + j) == iota((TOK, TOK), 1)).astype(F32).astype(BF)
    left = mm(pick, packed[...]).astype(BF)
    right = mm(pick, cot[...]).astype(BF)
    for k in range(8):
        outs[k][:, 0:256] = left[64 * k : 64 * k + 64]
        outs[k][:, 256 : 256 + MODEL] = right[64 * k : 64 * k + 64]
        outs[k][:, 256 + MODEL :] = jnp.zeros((64, 64), BF)


def row_forward_kernel(packed, w_in, out):
    aux = packed[...]
    values = mm(aux[:, :MODEL], w_in[:, :CHAN]).astype(BF).astype(F32)
    out[...] = scan_tokens(aux, values, True, True).astype(BF)


def gate_terms(aux, cot, w_in, w_out):
    gate = mm(aux[:, :MODEL], w_in[:, CHAN:]).astype(BF).astype(F32)
    sig = 1.0 / (1.0 + jnp.exp(-gate))
    return gate, sig, mm_t(cot, w_out[...])


def col_adjoint_kernel(place, row_out, w_in, w_out, *refs):
    pieces, (out, whole, tokens, scratch) = refs[:8], refs[8:]
    x, core = place[0] // 2, place[0] % 2
    for k in range(8):
        source = ((x + 4 - k // 2) % 4) * 2 + (core + k % 2) % 2
        whole[pl.ds(pl.multiple_of(source * 64, 64), 64), :] = pieces[k][...]
    aux = whole[:, :256]
    cot = whole[:, 256 : 256 + MODEL]
    gate, sig, hidden_grad = gate_terms(aux, cot, w_in, w_out)
    col_grad = (hidden_grad * gate * sig).astype(BF).astype(F32)
    row_grad = scan_tokens(aux, col_grad, False, False)
    split_lanes(tokens, row_out[...].astype(F32))
    to_columns(scratch, 0, tokens)
    split_lanes(tokens, row_grad)
    for l in range(3):
        for j in range(4):
            scratch[l, pl.ds(4 + j, 128, stride=8), :] = tokens[l, pl.ds(j, 128, stride=4), :]
    for l in range(3):
        out[:, 128 * l : 128 * l + 128] = scratch[l].astype(BF)


def second_kernel(came, whole, packed, w_in, w_out, block, partial, out, tokens, scratch):
    split_lanes(scratch, came[...].astype(F32))
    for l in range(3):
        for j in range(4):
            tokens[l, pl.ds(j, 128, stride=4), :] = scratch[l, pl.ds(j, 128, stride=8), :]
    row_out = jnp.concatenate([tokens[l] for l in range(3)], axis=1)
    for l in range(3):
        for r in range(8):
            for j in range(4):
                tokens[l, pl.ds(4 * r + j, 16, stride=32), :] = scratch[
                    l, pl.ds(r * 128 + 4 + j, 16, stride=8), :
                ]
    row_grad = jnp.concatenate([tokens[l] for l in range(3)], axis=1)

    aux = whole[:, :256]
    feat = whole[:, :MODEL]
    cot = whole[:, 256 : 256 + MODEL]
    col_out = scan_tokens(aux, row_out, False, True).astype(BF).astype(F32)
    gate, sig, hidden_grad = gate_terms(aux, cot, w_in, w_out)
    hidden = (col_out * gate * sig).astype(BF)
    block[...] = (feat.astype(F32) + mm(hidden, w_out[...])).astype(BF)
    gate_grad = (hidden_grad * col_out * sig * (1.0 + gate * (1.0 - sig))).astype(BF)
    partial[...] = cot.astype(F32) + mm_t(gate_grad, w_in[:, CHAN:])
    shifted = jnp.concatenate([jnp.zeros((TOK, MODEL), F32), cot.astype(F32)], axis=1).astype(BF)
    out_part = t_mm(hidden, shifted)
    gate_part = t_mm(feat, gate_grad)

    row_aux = packed[...]
    value_grad = scan_tokens(row_aux, row_grad, True, False).astype(BF)
    pull = mm_t(value_grad, w_in[:, :CHAN])
    pull = jnp.concatenate([pull, jnp.zeros((TOK, MODEL), F32)], axis=1)
    value_part = t_mm(row_aux[:, :MODEL], value_grad)

    split_lanes(tokens, pull)
    to_columns(scratch, 0, tokens)
    in_part = jnp.concatenate([value_part, gate_part], axis=0)
    for l in range(3):
        lanes = slice(128 * l, 128 * l + 128)
        for k in range(3):
            rows = slice(128 * k, 128 * k + 128)
            scratch[l, pl.ds(4 + k, 128, stride=8), :] = in_part[rows, lanes]
            if l > 0:
                scratch[l, pl.ds(k, 128, stride=8), :] += out_part[rows, lanes]
        scratch[l, pl.ds(7, 128, stride=8), :] = jnp.zeros((128, 128), F32)
    for l in range(3):
        out[:, 128 * l : 128 * l + 128] = scratch[l].astype(BF)


def third_kernel(place, came, partial, block, sums, *refs):
    outs, scratch, grad = refs[:8], refs[8], refs[9]
    x, core = place[0] // 2, place[0] % 2
    total = jnp.sum(came[...].astype(F32), axis=0) * (65536.0**-0.5)
    tiles = [total[4 + k : 5 + k, 128 * l : 128 * l + 128] for k in range(3) for l in range(3)]
    tiles += [total[k : k + 1, 128 * l : 128 * l + 128] for k in range(3) for l in (1, 2)]
    tiles.append(jnp.zeros((1, 128), F32))
    slice_ = jnp.concatenate(tiles, axis=0).astype(BF)
    sums[...] = jnp.broadcast_to(slice_[None], (128, 16, 128))
    for l in range(2):
        scratch[l] = came[:, :, 128 * l : 128 * l + 128].astype(F32).reshape(1024, 128)
    for l in range(2):
        for j in range(4):
            grad[l, pl.ds(j, 128, stride=4), :] = scratch[l, pl.ds(j, 128, stride=8), :]
    pull = jnp.concatenate([grad[0], grad[1][:, :64]], axis=1)
    whole = (partial[...] + pull).astype(BF)
    scratch[0, 0:TOK, :] = whole[:, 0:128].astype(F32)
    scratch[1, 0:TOK, 0:64] = whole[:, 128:192].astype(F32)
    for k in range(8):
        dest = ((x + k // 2) % 4) * 2 + (core + k % 2) % 2
        rows = pl.ds(pl.multiple_of(dest * 64, 64), 64)
        outs[k][:, 0:MODEL] = block[rows, :]
        outs[k][:, MODEL:256] = jnp.zeros((64, 64), BF)
        outs[k][:, 256:384] = scratch[0, rows, :].astype(BF)
        outs[k][:, 384:512] = scratch[1, rows, :].astype(BF)


def last_kernel(place, sums, *refs):
    pieces, (block, grad, in_grad, out_grad, piece, whole, weights) = refs[:8], refs[8:]
    x, core = place[0] // 2, place[0] % 2
    for k in range(8):
        source = ((x + 4 - k // 2) % 4) * 2 + (core + k % 2) % 2
        for l in range(4):
            piece[l] = pieces[k][:, 128 * l : 128 * l + 128].astype(F32)
            for j in range(4):
                whole[l, pl.ds(4 * source + j, 16, stride=32), :] = piece[
                    l, pl.ds(j, 16, stride=4), :
                ]
    block[:, 0:128] = whole[0].astype(BF)
    block[:, 128:192] = whole[1, :, 0:64].astype(BF)
    grad[:, 0:128] = whole[2].astype(BF)
    grad[:, 128:192] = whole[3, :, 0:64].astype(BF)
    weights[...] = sums[...].astype(F32)
    strided = lambda first: weights[pl.ds(first, 128, stride=16), :]
    for l in range(3):
        lanes = slice(128 * l, 128 * l + 128)
        gate_lanes = slice(CHAN + 128 * l, CHAN + 128 * l + 128)
        in_grad[0:128, lanes] = strided(l)
        middle = strided(3 + l)
        in_grad[128:192, lanes] = middle[0:64]
        in_grad[0:64, gate_lanes] = middle[64:128]
        in_grad[64:192, gate_lanes] = strided(6 + l)
    lane = iota((128, 128), 1)
    for k in range(3):
        first = pltpu.roll(strided(9 + 2 * k), 64, 1)
        second = pltpu.roll(strided(10 + 2 * k), 64, 1)
        out_grad[128 * k : 128 * k + 128, 0:128] = jnp.where(lane < 64, first, second)
        out_grad[128 * k : 128 * k + 128, 128:192] = second[:, 0:64]


def call(kernel, outs, ins, scratch=(), flops=10**8):
    specs = [pl.BlockSpec(memory_space=pltpu.VMEM)] * len(ins)
    if ins[0].shape == (1,):
        specs[0] = pl.BlockSpec(memory_space=pltpu.SMEM)
    return pl.pallas_call(
        kernel,
        out_shape=[jax.ShapeDtypeStruct(shape, dtype) for shape, dtype in outs],
        in_specs=specs,
        out_specs=[pl.BlockSpec(memory_space=pltpu.VMEM)] * len(outs),
        scratch_shapes=[pltpu.VMEM(shape, dtype) for shape, dtype in scratch],
        compiler_params=pltpu.CompilerParams(vmem_limit_bytes=VMEM_LIMIT),
        cost_estimate=pl.CostEstimate(flops=flops, bytes_accessed=10**6, transcendentals=10**5),
    )(*ins)


def row_pairs(k):
    return [(i, ((i // 2 + k // 2) % 4) * 2 + (i + k) % 2) for i in range(8)]


def swap_rows(pieces):
    return [pieces[0]] + [lax.ppermute(pieces[k], "row", row_pairs(k)) for k in range(1, 8)]


def on_device(features, selectors, log_decay, in_weight, out_weight, cotangent):
    place = lax.axis_index("row").astype(jnp.int32).reshape(1)
    pad = jnp.zeros((16, 32, 26), BF)
    flat_sel = selectors.reshape(16, 32, 64)
    row_packed = jnp.concatenate(
        [features, flat_sel[:, :, 0:32], log_decay[:, :, 0], pad], axis=-1
    )
    col_packed = jnp.concatenate(
        [features, flat_sel[:, :, 32:64], log_decay[:, :, 1], pad], axis=-1
    )
    row_packed = lax.all_to_all(row_packed, "col", 0, 0).reshape(TOK, 256)
    piece = ((64, 512), BF)
    pieces = call(
        send_rows_kernel,
        [piece] * 8,
        [place, col_packed.reshape(TOK, 256), cotangent.reshape(TOK, MODEL)],
    )
    pieces = swap_rows(pieces)
    (row_out,) = call(row_forward_kernel, [((TOK, CHAN), BF)], [row_packed, in_weight])
    wide = ((3, 1024, 128), F32)
    tall = ((3, TOK, 128), F32)
    sent, whole = call(
        col_adjoint_kernel,
        [((1024, CHAN), BF), ((TOK, 512), BF)],
        [place, row_out, in_weight, out_weight, *pieces],
        [tall, wide],
    )
    came = lax.all_to_all(sent.reshape(128, 8, CHAN), ("row", "col"), 0, 0)
    block, partial, sent = call(
        second_kernel,
        [((TOK, MODEL), BF), ((TOK, MODEL), F32), ((1024, CHAN), BF)],
        [came.reshape(1024, CHAN), whole, row_packed, in_weight, out_weight],
        [tall, wide],
    )
    came = lax.all_to_all(sent.reshape(128, 8, CHAN), ("row", "col"), 0, 0)
    sums, *pieces = call(
        third_kernel,
        [((128, 16, 128), BF)] + [piece] * 8,
        [place, came, partial, block],
        [((2, 1024, 128), F32), ((2, TOK, 128), F32)],
    )
    sums = lax.all_to_all(sums, ("row", "col"), 0, 0).reshape(2048, 128)
    pieces = swap_rows(pieces)
    block, grad, in_grad, out_grad = call(
        last_kernel,
        [((TOK, MODEL), BF), ((TOK, MODEL), BF), ((MODEL, 2 * CHAN), F32), ((CHAN, MODEL), F32)],
        [place, sums, *pieces],
        [((4, 64, 128), F32), ((4, TOK, 128), F32), ((2048, 128), F32)],
    )
    return (block.reshape(16, 32, MODEL), grad.reshape(16, 32, MODEL), in_grad, out_grad)


def solution(mesh):
    in_specs = (
        P("row", "col", None),
        P("row", "col", None, None),
        P("row", "col", None, None),
        P(),
        P(),
        P("row", "col", None),
    )
    out_specs = (P("row", "col", None), P("row", "col", None), P(), P())
    return jax.shard_map(
        on_device, mesh=mesh, in_specs=in_specs, out_specs=out_specs, check_vma=False
    )
```

```python
import jax
import jax.numpy as jnp
from jax import lax
from jax.experimental import pallas as pl
from jax.experimental.pallas import tpu as pltpu
from jax.sharding import PartitionSpec as P

BF = jnp.bfloat16
F32 = jnp.float32
MODEL = 192
CHAN = 384
TOK = 512
GROUP = 256
VMEM_LIMIT = 48 * 1024 * 1024


def iota(shape, dim):
    return lax.broadcasted_iota(jnp.int32, shape, dim)


def mm(a, b):
    return jnp.dot(a, b, preferred_element_type=F32)


def mm_t(a, b):
    return lax.dot_general(a, b, (((1,), (1,)), ((), ())), preferred_element_type=F32)


def t_mm(a, b):
    return lax.dot_general(a, b, (((0,), (0,)), ((), ())), preferred_element_type=F32)


def spread(aux, first):
    pick = (iota((256, 128), 0) - first == iota((256, 128), 1) % 16).astype(F32).astype(BF)
    return mm(aux, pick)


HALVES = (slice(0, GROUP), slice(GROUP, TOK))


def prepare_scan(aux, by_row, forward):
    token = iota((TOK, 128), 0)
    chunk = token // 64 if by_row else (token // GROUP) * 4 + token % 4
    member = (iota((TOK, 128), 1) // 16 == chunk).astype(F32)
    b_part = (spread(aux, 192) * member).astype(BF)
    c_part = (spread(aux, 208) * member).astype(BF)
    heads = (iota((256, CHAN), 0) - 224 == iota((256, CHAN), 1) // 64).astype(F32).astype(BF)
    log_step = mm(aux, heads).astype(BF)
    here, there = iota((GROUP, GROUP), 0), iota((GROUP, GROUP), 1)
    same = (here // 64 == there // 64) if by_row else (here % 4 == there % 4)
    if forward:
        order, counted, src, out = there <= here, there <= here, b_part, c_part
    else:
        order, counted, src, out = there >= here, there > here, c_part, b_part
    add_up = (same & counted).astype(F32).astype(BF)
    run = jnp.concatenate([mm(add_up, log_step[h]) for h in HALVES], axis=0)
    decay = jnp.exp(t_mm(member.astype(BF), log_step))
    scores = [jnp.where(order, mm_t(out[h], src[h]), 0.0).astype(BF) for h in HALVES]
    return jnp.concatenate(scores, axis=0), src, out, jnp.exp(-run), jnp.exp(run), decay


def apply_scan(prepared, values, by_row, forward):
    scores, src, out, up, down, decay = prepared
    raised = (up[...] * values).astype(BF)
    states = t_mm(src[...], raised)
    zero = jnp.zeros((16, CHAN), F32)
    carried = [zero] * 8
    part = lambda array, k: array[16 * k : 16 * k + 16]
    if by_row:
        steps = [(k, k + 1) for k in range(7)] if forward else [(k, k - 1) for k in range(7, 0, -1)]
    else:
        steps = [(j, j + 4) for j in range(4)] if forward else [(j + 4, j) for j in range(4)]
    for old, new in steps:
        carried[new] = part(decay, old) * (carried[old] + part(states, old))
    coming = jnp.concatenate(carried, axis=0).astype(BF)
    inner = jnp.concatenate([mm(scores[h, :], raised[h]) for h in HALVES], axis=0)
    return down[...] * (inner + mm(out[...], coming))


def scan_tokens(aux, values, by_row, forward):
    return apply_scan(prepare_scan(aux, by_row, forward), values, by_row, forward)


def to_columns(scratch, slot, token_rows):
    for l in range(CHAN // 128):
        for r in range(8):
            for j in range(4):
                scratch[l, pl.ds(r * 128 + slot + j, 16, stride=8), :] = token_rows[
                    l, pl.ds(4 * r + j, 16, stride=32), :
                ]


def split_lanes(ref, value):
    for l in range(value.shape[1] // 128):
        ref[l] = value[:, 128 * l : 128 * l + 128]


def peers(place, k):
    x, core = place[0] // 2, place[0] % 2
    return ((x + k // 2) % 4) * 2 + (core + k % 2) % 2


def with_aux(feat, sel, log, slot):
    index, lane = iota((48, 128), 0), iota((48, 128), 1)
    pick = ((lane == index + 64) & (index < 38)).astype(F32).astype(BF)
    blank = jnp.zeros((10, 32), F32)
    aux = []
    for i in range(16):
        chosen = sel[i, 32 * slot : 32 * slot + 32, :].astype(F32)
        decay = log[i].astype(F32)[:, slot, :]
        aux.append(t_mm(jnp.concatenate([chosen, decay, blank], axis=0).astype(BF), pick))
    upper = feat[:, 128:MODEL].astype(F32)
    upper = jnp.concatenate([upper, jnp.zeros((TOK, 64), F32)], axis=1)
    return (upper + jnp.concatenate(aux, axis=0)).astype(BF)


def pack_rows_kernel(feat, sel, log, packed):
    packed[:, 0:128] = feat[:, 0:128]
    packed[:, 128:256] = with_aux(feat, sel, log, 0)


def pack_columns_kernel(place, feat, cot, sel, log, *outs):
    slot = iota((TOK, 1), 0)
    row, j = (slot % 64) // 4, slot % 4
    dest = peers(place, slot // 64)
    choose = ((row * 32 + 4 * dest + j) == iota((TOK, TOK), 1)).astype(F32).astype(BF)
    left = mm(choose, feat[:, 0:128]).astype(BF)
    middle = mm(choose, with_aux(feat, sel, log, 1)).astype(BF)
    right = mm(choose, cot[...]).astype(BF)
    for k in range(8):
        rows = slice(64 * k, 64 * k + 64)
        outs[k][:, 0:128] = left[rows]
        outs[k][:, 128:256] = middle[rows]
        outs[k][:, 256 : 256 + MODEL] = right[rows]
        outs[k][:, 256 + MODEL :] = jnp.zeros((64, 64), BF)


def row_forward_kernel(packed, w_in, out):
    aux = packed[...]
    values = mm(aux[:, :MODEL], w_in[:, :CHAN]).astype(BF).astype(F32)
    out[...] = scan_tokens(aux, values, True, True).astype(BF)


def gate_terms(aux, cot, w_in, w_out):
    gate = mm(aux[:, :MODEL], w_in[:, CHAN:]).astype(BF).astype(F32)
    sig = 1.0 / (1.0 + jnp.exp(-gate))
    return gate, sig, mm(cot, w_out[...])


def sender(place, k):
    x, core = place[0] // 2, place[0] % 2
    return ((x + 4 - k // 2) % 4) * 2 + (core + k % 2) % 2


def col_adjoint_kernel(place, row_out, w_in, w_out, *refs):
    pieces, (out, whole, tokens, scratch) = refs[:8], refs[8:]
    for k in range(8):
        whole[pl.ds(pl.multiple_of(sender(place, k) * 64, 64), 64), :] = pieces[k][...]
    aux = whole[:, :256]
    cot = whole[:, 256 : 256 + MODEL]
    gate, sig, hidden_grad = gate_terms(aux, cot, w_in, w_out)
    col_grad = (hidden_grad * gate * sig).astype(BF).astype(F32)
    row_grad = scan_tokens(aux, col_grad, False, False)
    split_lanes(tokens, row_out[...].astype(F32))
    to_columns(scratch, 0, tokens)
    split_lanes(tokens, row_grad)
    for l in range(3):
        for j in range(4):
            scratch[l, pl.ds(4 + j, 128, stride=8), :] = tokens[l, pl.ds(j, 128, stride=4), :]
    for l in range(3):
        out[:, 128 * l : 128 * l + 128] = scratch[l].astype(BF)


def second_kernel(came, whole, packed, w_in, w_out, block, partial, out, tokens, scratch):
    split_lanes(scratch, came[...].astype(F32))
    for l in range(3):
        for j in range(4):
            tokens[l, pl.ds(j, 128, stride=4), :] = scratch[l, pl.ds(j, 128, stride=8), :]
    row_out = jnp.concatenate([tokens[l] for l in range(3)], axis=1)
    feat = whole[:, :MODEL]
    cot = whole[:, 256 : 256 + MODEL]
    col_out = scan_tokens(whole[:, :256], row_out, False, True).astype(BF).astype(F32)
    gate, sig, hidden_grad = gate_terms(feat, cot, w_in, w_out)
    hidden = (col_out * gate * sig).astype(BF)
    block[...] = feat.astype(F32) + mm_t(hidden, w_out[...])
    gate_grad = (hidden_grad * col_out * sig * (1.0 + gate * (1.0 - sig))).astype(BF)
    partial[...] = cot.astype(F32) + mm_t(gate_grad, w_in[:, CHAN:])
    shifted = jnp.concatenate([jnp.zeros((TOK, MODEL), F32), cot.astype(F32)], axis=1).astype(BF)
    out_part = t_mm(hidden, shifted)
    gate_part = t_mm(feat, gate_grad)

    for l in range(3):
        for r in range(8):
            for j in range(4):
                tokens[l, pl.ds(4 * r + j, 16, stride=32), :] = scratch[
                    l, pl.ds(r * 128 + 4 + j, 16, stride=8), :
                ]
    row_grad = jnp.concatenate([tokens[l] for l in range(3)], axis=1)
    value_grad = scan_tokens(packed[...], row_grad, True, False).astype(BF)
    pull = mm_t(value_grad, w_in[:, :CHAN])
    pull = jnp.concatenate([pull, jnp.zeros((TOK, MODEL), F32)], axis=1)
    value_part = t_mm(packed[:, :MODEL], value_grad)

    split_lanes(tokens, pull)
    to_columns(scratch, 0, tokens)
    in_part = jnp.concatenate([value_part, gate_part], axis=0)
    for l in range(3):
        lanes = slice(128 * l, 128 * l + 128)
        for k in range(3):
            rows = slice(128 * k, 128 * k + 128)
            scratch[l, pl.ds(4 + k, 128, stride=8), :] = in_part[rows, lanes]
            if l > 0:
                scratch[l, pl.ds(k, 128, stride=8), :] += out_part[rows, lanes]
        scratch[l, pl.ds(7, 128, stride=8), :] = jnp.zeros((128, 128), F32)
    for l in range(3):
        out[:, 128 * l : 128 * l + 128] = scratch[l].astype(BF)


def sum_kernel(came, sums):
    total = jnp.sum(came[...].astype(F32), axis=0) * (65536.0**-0.5)
    tiles = [total[4 + k : 5 + k, 128 * l : 128 * l + 128] for k in range(3) for l in range(3)]
    tiles += [total[k : k + 1, 128 * l : 128 * l + 128] for k in range(3) for l in (1, 2)]
    tiles.append(jnp.zeros((1, 128), F32))
    slice_ = jnp.concatenate(tiles, axis=0).astype(BF)
    sums[...] = jnp.broadcast_to(slice_[None], (128, 16, 128))


def return_kernel(place, came, partial, block, *refs):
    outs, (scratch, grad, whole) = refs[:8], refs[8:]
    for l in range(2):
        scratch[l] = came[:, :, 128 * l : 128 * l + 128].astype(F32).reshape(1024, 128)
    for l in range(2):
        for j in range(4):
            grad[l, pl.ds(j, 128, stride=4), :] = scratch[l, pl.ds(j, 128, stride=8), :]
    pull = jnp.concatenate([grad[0], grad[1][:, :64]], axis=1)
    whole[...] = jnp.concatenate([block[...], partial[...] + pull], axis=1).astype(BF)
    for k in range(8):
        rows = pl.ds(pl.multiple_of(peers(place, k) * 64, 64), 64)
        outs[k][...] = whole[rows, :]


def tokens_kernel(place, *refs):
    pieces, (block, grad, part, whole) = refs[:8], refs[8:]
    for k in range(8):
        first = 4 * sender(place, k)
        split_lanes(part, pieces[k][...].astype(F32))
        for l in range(3):
            for j in range(4):
                whole[l, pl.ds(first + j, 16, stride=32), :] = part[l, pl.ds(j, 16, stride=4), :]
    middle = whole[1]
    block[...] = jnp.concatenate([whole[0], middle[:, :64]], axis=1).astype(BF)
    grad[...] = jnp.concatenate([middle[:, 64:], whole[2]], axis=1).astype(BF)


def weights_kernel(sums, in_grad, out_grad, weights):
    weights[...] = sums[...].astype(F32)
    strided = lambda first: weights[pl.ds(first, 128, stride=16), :]
    for l in range(3):
        lanes = slice(128 * l, 128 * l + 128)
        gate_lanes = slice(CHAN + 128 * l, CHAN + 128 * l + 128)
        in_grad[0:128, lanes] = strided(l)
        middle = strided(3 + l)
        in_grad[128:192, lanes] = middle[0:64]
        in_grad[0:64, gate_lanes] = middle[64:128]
        in_grad[64:192, gate_lanes] = strided(6 + l)
    for k in range(3):
        lanes = slice(128 * k, 128 * k + 128)
        out_grad[0:64, lanes] = strided(9 + 2 * k).T[64:128]
        out_grad[64:192, lanes] = strided(10 + 2 * k).T


def call(kernel, outs, ins, scratch=(), flops=10**8, vmem=VMEM_LIMIT):
    specs = [pl.BlockSpec()] * len(ins)
    if ins[0].shape == (1,):
        specs[0] = pl.BlockSpec(memory_space=pltpu.SMEM)
    return pl.pallas_call(
        kernel,
        out_shape=[jax.ShapeDtypeStruct(shape, dtype) for shape, dtype in outs],
        in_specs=specs,
        out_specs=[pl.BlockSpec()] * len(outs),
        scratch_shapes=[pltpu.VMEM(shape, dtype) for shape, dtype in scratch],
        compiler_params=pltpu.CompilerParams(vmem_limit_bytes=vmem),
        cost_estimate=pl.CostEstimate(flops=flops, bytes_accessed=10**6, transcendentals=10**5),
    )(*ins)


def swap_rows(pieces):
    pairs = lambda k: [(i, ((i // 2 + k // 2) % 4) * 2 + (i + k) % 2) for i in range(8)]
    return [pieces[0]] + [lax.ppermute(pieces[k], "row", pairs(k)) for k in range(1, 8)]


def on_device(features, selectors, log_decay, in_weight, out_weight, cotangent):
    place = lax.axis_index("row").astype(jnp.int32).reshape(1)
    out_turned = out_weight.T
    feat = features.reshape(TOK, MODEL)
    sel = selectors.transpose(0, 2, 3, 1).reshape(16, 64, 32)
    log = log_decay.transpose(0, 3, 2, 1)
    wide = ((3, 1024, 128), F32)
    tall = ((3, TOK, 128), F32)
    (row_packed,) = call(
        pack_rows_kernel, [((TOK, 256), BF)], [feat, sel, log], vmem=60 * 1024 * 1024
    )
    row_packed = lax.all_to_all(row_packed.reshape(16, 32, 256), "col", 0, 0).reshape(TOK, 256)
    pieces = call(
        pack_columns_kernel,
        [((64, 512), BF)] * 8,
        [place, feat, cotangent.reshape(TOK, MODEL), sel, log],
    )
    pieces = swap_rows(pieces)
    (row_out,) = call(row_forward_kernel, [((TOK, CHAN), BF)], [row_packed, in_weight])
    sent, whole = call(
        col_adjoint_kernel,
        [((1024, CHAN), BF), ((TOK, 512), BF)],
        [place, row_out, in_weight, out_turned, *pieces],
        [tall, wide],
    )
    came = lax.all_to_all(sent.reshape(128, 8, CHAN), ("row", "col"), 0, 0)
    block, partial, sent = call(
        second_kernel,
        [((TOK, MODEL), F32), ((TOK, MODEL), F32), ((1024, CHAN), BF)],
        [came.reshape(1024, CHAN), whole, row_packed, in_weight, out_turned],
        [tall, wide],
    )
    came = lax.all_to_all(sent.reshape(128, 8, CHAN), ("row", "col"), 0, 0)
    (sums,) = call(sum_kernel, [((128, 16, 128), BF)], [came])
    sums = lax.all_to_all(sums, ("row", "col"), 0, 0).reshape(2048, 128)
    pieces = call(
        return_kernel,
        [((64, CHAN), BF)] * 8,
        [place, came, partial, block],
        [((2, 1024, 128), F32), ((2, TOK, 128), F32), ((TOK, CHAN), BF)],
    )
    block, grad = call(
        tokens_kernel,
        [((TOK, MODEL), BF)] * 2,
        [place, *swap_rows(pieces)],
        [((3, 64, 128), F32), tall],
    )
    in_grad, out_grad = call(
        weights_kernel,
        [((MODEL, 2 * CHAN), F32), ((MODEL, CHAN), F32)],
        [sums],
        [((2048, 128), F32)],
    )
    return (block.reshape(16, 32, MODEL), grad.reshape(16, 32, MODEL), in_grad, out_grad.T)


def solution(mesh):
    in_specs = (
        P("row", "col", None),
        P("row", "col", None, None),
        P("row", "col", None, None),
        P(),
        P(),
        P("row", "col", None),
    )
    out_specs = (P("row", "col", None), P("row", "col", None), P(), P())
    return jax.shard_map(
        on_device, mesh=mesh, in_specs=in_specs, out_specs=out_specs, check_vma=False
    )
```

```python
import jax
import jax.numpy as jnp
from jax import lax
from jax.experimental import pallas as pl
from jax.experimental.pallas import tpu as pltpu
from jax.sharding import PartitionSpec as P

BF = jnp.bfloat16
F32 = jnp.float32
MODEL = 192
CHAN = 384
TOK = 512
GROUP = 256
VMEM_LIMIT = 48 * 1024 * 1024


def iota(shape, dim):
    return lax.broadcasted_iota(jnp.int32, shape, dim)


def mm(a, b):
    return jnp.dot(a, b, preferred_element_type=F32)


def mm_t(a, b):
    return lax.dot_general(a, b, (((1,), (1,)), ((), ())), preferred_element_type=F32)


def t_mm(a, b):
    return lax.dot_general(a, b, (((0,), (0,)), ((), ())), preferred_element_type=F32)


HALVES = (slice(0, GROUP), slice(GROUP, TOK))


def prepare_scan(aux, by_row, forward):
    token = iota((TOK, 128), 0)
    chunk = token // 64 if by_row else (token // GROUP) * 4 + token % 4
    member = (iota((TOK, 128), 1) // 16 == chunk).astype(F32)
    lane = iota((256, 640), 1)
    wanted = jnp.where(lane < 128, 192 + lane % 16, 208 + lane % 16)
    wanted = jnp.where(lane < 256, wanted, 220 + lane // 64)
    spread = mm(aux, (iota((256, 640), 0) == wanted).astype(F32).astype(BF))
    b_part = (spread[:, 0:128] * member).astype(BF)
    c_part = (spread[:, 128:256] * member).astype(BF)
    log_step = spread[:, 256:].astype(BF)
    here, there = iota((GROUP, GROUP), 0), iota((GROUP, GROUP), 1)
    same = (here // 64 == there // 64) if by_row else (here % 4 == there % 4)
    if forward:
        order, counted, src, out = there <= here, there <= here, b_part, c_part
    else:
        order, counted, src, out = there >= here, there > here, c_part, b_part
    add_up = (same & counted).astype(F32).astype(BF)
    run = jnp.concatenate([mm(add_up, log_step[h]) for h in HALVES], axis=0)
    decay = jnp.exp(t_mm(member.astype(BF), log_step))
    scores = [jnp.where(order, mm_t(out[h], src[h]), 0.0).astype(BF) for h in HALVES]
    return jnp.concatenate(scores, axis=0), src, out, jnp.exp(-run), jnp.exp(run), decay


def apply_scan(prepared, values, by_row, forward):
    scores, src, out, up, down, decay = prepared
    raised = (up[...] * values).astype(BF)
    states = t_mm(src[...], raised)
    zero = jnp.zeros((16, CHAN), F32)
    carried = [zero] * 8
    part = lambda array, k: array[16 * k : 16 * k + 16]
    if by_row:
        steps = [(k, k + 1) for k in range(7)] if forward else [(k, k - 1) for k in range(7, 0, -1)]
    else:
        steps = [(j, j + 4) for j in range(4)] if forward else [(j + 4, j) for j in range(4)]
    for old, new in steps:
        carried[new] = part(decay, old) * (carried[old] + part(states, old))
    coming = jnp.concatenate(carried, axis=0).astype(BF)
    inner = jnp.concatenate([mm(scores[h, :], raised[h]) for h in HALVES], axis=0)
    return down[...] * (inner + mm(out[...], coming))


def scan_tokens(aux, values, by_row, forward):
    return apply_scan(prepare_scan(aux, by_row, forward), values, by_row, forward)


def to_columns(scratch, slot, token_rows):
    for l in range(CHAN // 128):
        for r in range(8):
            for j in range(4):
                scratch[l, pl.ds(r * 128 + slot + j, 16, stride=8), :] = token_rows[
                    l, pl.ds(4 * r + j, 16, stride=32), :
                ]


def split_lanes(ref, value):
    for l in range(value.shape[1] // 128):
        ref[l] = value[:, 128 * l : 128 * l + 128]


def peers(place, k):
    x, core = place[0] // 2, place[0] % 2
    return ((x + k // 2) % 4) * 2 + (core + k % 2) % 2


def with_aux(feat, sel, log, slot):
    index, lane = iota((48, 128), 0), iota((48, 128), 1)
    pick = ((lane == index + 64) & (index < 38)).astype(F32).astype(BF)
    blank = jnp.zeros((10, 32), F32)
    aux = []
    for i in range(16):
        chosen = sel[i, 32 * slot : 32 * slot + 32, :].astype(F32)
        decay = log[i].astype(F32)[:, slot, :]
        aux.append(t_mm(jnp.concatenate([chosen, decay, blank], axis=0).astype(BF), pick))
    upper = feat[:, 128:MODEL].astype(F32)
    upper = jnp.concatenate([upper, jnp.zeros((TOK, 64), F32)], axis=1)
    return (upper + jnp.concatenate(aux, axis=0)).astype(BF)


def pack_rows_kernel(feat, sel, log, packed):
    packed[:, 0:128] = feat[:, 0:128]
    packed[:, 128:256] = with_aux(feat, sel, log, 0)


def pack_columns_kernel(place, feat, cot, sel, log, *outs):
    slot = iota((TOK, 1), 0)
    row, j = (slot % 64) // 4, slot % 4
    dest = peers(place, slot // 64)
    choose = ((row * 32 + 4 * dest + j) == iota((TOK, TOK), 1)).astype(F32).astype(BF)
    left = mm(choose, feat[:, 0:128]).astype(BF)
    middle = mm(choose, with_aux(feat, sel, log, 1)).astype(BF)
    right = mm(choose, cot[...]).astype(BF)
    for k in range(4):
        rows = slice(128 * k, 128 * k + 128)
        outs[k][:, 0:128] = left[rows]
        outs[k][:, 128:256] = middle[rows]
        outs[k][:, 256 : 256 + MODEL] = right[rows]
        outs[k][:, 256 + MODEL :] = jnp.zeros((128, 64), BF)


def row_forward_kernel(packed, w_in, out):
    aux = packed[...]
    values = mm(aux[:, :MODEL], w_in[:, :CHAN]).astype(BF).astype(F32)
    out[...] = scan_tokens(aux, values, True, True).astype(BF)


def gate_terms(aux, cot, w_in, w_out):
    gate = mm(aux[:, :MODEL], w_in[:, CHAN:]).astype(BF).astype(F32)
    sig = 1.0 / (1.0 + jnp.exp(-gate))
    return gate, sig, mm(cot, w_out[...])


def sender(place, k):
    x, core = place[0] // 2, place[0] % 2
    return ((x + 4 - k // 2) % 4) * 2 + (core + k % 2) % 2


def col_adjoint_kernel(place, row_out, w_in, w_out, *refs):
    pieces, (out, whole, tokens, scratch) = refs[:8], refs[8:]
    for k in range(8):
        half, first = k % 2, 64 * (k % 2)
        rows = pl.ds(pl.multiple_of(sender(place, k) * 64, 64), 64)
        whole[rows, :] = pieces[4 * half + k // 2][first : first + 64, :]
    aux = whole[:, :256]
    cot = whole[:, 256 : 256 + MODEL]
    gate, sig, hidden_grad = gate_terms(aux, cot, w_in, w_out)
    col_grad = (hidden_grad * gate * sig).astype(BF).astype(F32)
    row_grad = scan_tokens(aux, col_grad, False, False)
    split_lanes(tokens, row_out[...].astype(F32))
    to_columns(scratch, 0, tokens)
    split_lanes(tokens, row_grad)
    for l in range(3):
        for j in range(4):
            scratch[l, pl.ds(4 + j, 128, stride=8), :] = tokens[l, pl.ds(j, 128, stride=4), :]
    for l in range(3):
        out[:, 128 * l : 128 * l + 128] = scratch[l].astype(BF)


def second_kernel(came, whole, packed, w_in, w_out, block, partial, out, tokens, scratch):
    split_lanes(scratch, came[...].astype(F32))
    for l in range(3):
        for j in range(4):
            tokens[l, pl.ds(j, 128, stride=4), :] = scratch[l, pl.ds(j, 128, stride=8), :]
    row_out = jnp.concatenate([tokens[l] for l in range(3)], axis=1)
    feat = whole[:, :MODEL]
    cot = whole[:, 256 : 256 + MODEL]
    col_out = scan_tokens(whole[:, :256], row_out, False, True).astype(BF).astype(F32)
    gate, sig, hidden_grad = gate_terms(feat, cot, w_in, w_out)
    hidden = (col_out * gate * sig).astype(BF)
    block[...] = feat.astype(F32) + mm_t(hidden, w_out[...])
    gate_grad = (hidden_grad * col_out * sig * (1.0 + gate * (1.0 - sig))).astype(BF)
    partial[...] = cot.astype(F32) + mm_t(gate_grad, w_in[:, CHAN:])
    shifted = jnp.concatenate([jnp.zeros((TOK, MODEL), F32), cot.astype(F32)], axis=1).astype(BF)
    out_part = t_mm(hidden, shifted)
    gate_part = t_mm(feat, gate_grad)

    for l in range(3):
        for r in range(8):
            for j in range(4):
                tokens[l, pl.ds(4 * r + j, 16, stride=32), :] = scratch[
                    l, pl.ds(r * 128 + 4 + j, 16, stride=8), :
                ]
    row_grad = jnp.concatenate([tokens[l] for l in range(3)], axis=1)
    value_grad = scan_tokens(packed[...], row_grad, True, False).astype(BF)
    pull = mm_t(value_grad, w_in[:, :CHAN])
    pull = jnp.concatenate([pull, jnp.zeros((TOK, MODEL), F32)], axis=1)
    value_part = t_mm(packed[:, :MODEL], value_grad)

    split_lanes(tokens, pull)
    to_columns(scratch, 0, tokens)
    in_part = jnp.concatenate([value_part, gate_part], axis=0)
    for l in range(3):
        lanes = slice(128 * l, 128 * l + 128)
        for k in range(3):
            rows = slice(128 * k, 128 * k + 128)
            scratch[l, pl.ds(4 + k, 128, stride=8), :] = in_part[rows, lanes]
            if l > 0:
                scratch[l, pl.ds(k, 128, stride=8), :] += out_part[rows, lanes]
        scratch[l, pl.ds(7, 128, stride=8), :] = jnp.zeros((128, 128), F32)
    for l in range(3):
        out[:, 128 * l : 128 * l + 128] = scratch[l].astype(BF)


def sum_kernel(came, sums):
    total = jnp.sum(came[...].astype(F32), axis=0) * (65536.0**-0.5)
    tiles = [total[4 + k : 5 + k, 128 * l : 128 * l + 128] for k in range(3) for l in range(3)]
    tiles += [total[k : k + 1, 128 * l : 128 * l + 128] for k in range(3) for l in (1, 2)]
    tiles.append(jnp.zeros((1, 128), F32))
    slice_ = jnp.concatenate(tiles, axis=0).astype(BF)
    sums[...] = jnp.broadcast_to(slice_[None], (128, 16, 128))


def return_kernel(place, came, partial, block, *refs):
    outs, (scratch, grad, whole) = refs[:8], refs[8:]
    for l in range(2):
        scratch[l] = came[:, :, 128 * l : 128 * l + 128].astype(F32).reshape(1024, 128)
    for l in range(2):
        for j in range(4):
            grad[l, pl.ds(j, 128, stride=4), :] = scratch[l, pl.ds(j, 128, stride=8), :]
    pull = jnp.concatenate([grad[0], grad[1][:, :64]], axis=1)
    whole[...] = jnp.concatenate([block[...], partial[...] + pull], axis=1).astype(BF)
    for k in range(8):
        rows = pl.ds(pl.multiple_of(peers(place, k) * 64, 64), 64)
        outs[k][...] = whole[rows, :]


def last_kernel(place, sums, *refs):
    pieces, (block, grad, in_grad, out_grad, part, whole, weights) = refs[:8], refs[8:]
    weights[...] = sums[...].astype(F32)
    strided = lambda first: weights[pl.ds(first, 128, stride=16), :]
    for l in range(3):
        lanes = slice(128 * l, 128 * l + 128)
        gate_lanes = slice(CHAN + 128 * l, CHAN + 128 * l + 128)
        in_grad[0:128, lanes] = strided(l)
        middle = strided(3 + l)
        in_grad[128:192, lanes] = middle[0:64]
        in_grad[0:64, gate_lanes] = middle[64:128]
        in_grad[64:192, gate_lanes] = strided(6 + l)
    for k in range(3):
        lanes = slice(128 * k, 128 * k + 128)
        out_grad[0:64, lanes] = strided(9 + 2 * k).T[64:128]
        out_grad[64:192, lanes] = strided(10 + 2 * k).T
    for k in range(8):
        first = 4 * sender(place, k)
        split_lanes(part.at[k], pieces[k][...].astype(F32))
        for l in range(3):
            for j in range(4):
                whole[l, pl.ds(first + j, 16, stride=32), :] = part[k, l, pl.ds(j, 16, stride=4), :]
    middle = whole[1]
    block[...] = jnp.concatenate([whole[0], middle[:, :64]], axis=1).astype(BF)
    grad[...] = jnp.concatenate([middle[:, 64:], whole[2]], axis=1).astype(BF)


def call(kernel, outs, ins, scratch=(), flops=10**8, vmem=VMEM_LIMIT):
    specs = [pl.BlockSpec()] * len(ins)
    if ins[0].shape == (1,):
        specs[0] = pl.BlockSpec(memory_space=pltpu.SMEM)
    return pl.pallas_call(
        kernel,
        out_shape=[jax.ShapeDtypeStruct(shape, dtype) for shape, dtype in outs],
        in_specs=specs,
        out_specs=[pl.BlockSpec()] * len(outs),
        scratch_shapes=[pltpu.VMEM(shape, dtype) for shape, dtype in scratch],
        compiler_params=pltpu.CompilerParams(vmem_limit_bytes=vmem),
        cost_estimate=pl.CostEstimate(flops=flops, bytes_accessed=10**6, transcendentals=10**5),
    )(*ins)


def swap_rows(pieces):
    pairs = lambda k: [(i, ((i // 2 + k // 2) % 4) * 2 + (i + k) % 2) for i in range(8)]
    return [pieces[0]] + [lax.ppermute(pieces[k], "row", pairs(k)) for k in range(1, 8)]


def swap_rows_in_steps(pieces):
    along = lambda s: [(i, (i + 2 * s) % 8) for i in range(8)]
    mine = [pieces[0]] + [lax.ppermute(pieces[s], "row", along(s)) for s in (1, 2, 3)]
    return mine + [lax.ppermute(piece, "row", [(i, i ^ 1) for i in range(8)]) for piece in mine]


def on_device(features, selectors, log_decay, in_weight, out_weight, cotangent):
    place = lax.axis_index("row").astype(jnp.int32).reshape(1)
    out_turned = out_weight.T
    feat = features.reshape(TOK, MODEL)
    sel = selectors.transpose(0, 2, 3, 1).reshape(16, 64, 32)
    log = log_decay.transpose(0, 3, 2, 1)
    wide = ((3, 1024, 128), F32)
    tall = ((3, TOK, 128), F32)
    (row_packed,) = call(
        pack_rows_kernel, [((TOK, 256), BF)], [feat, sel, log], vmem=60 * 1024 * 1024
    )
    row_packed = lax.all_to_all(row_packed.reshape(16, 32, 256), "col", 0, 0).reshape(TOK, 256)
    pieces = call(
        pack_columns_kernel,
        [((128, 512), BF)] * 4,
        [place, feat, cotangent.reshape(TOK, MODEL), sel, log],
    )
    pieces = swap_rows_in_steps(pieces)
    (row_out,) = call(
        row_forward_kernel, [((TOK, CHAN), BF)], [row_packed, in_weight], flops=3 * 10**10
    )
    sent, whole = call(
        col_adjoint_kernel,
        [((1024, CHAN), BF), ((TOK, 512), BF)],
        [place, row_out, in_weight, out_turned, *pieces],
        [tall, wide],
    )
    came = lax.all_to_all(sent.reshape(128, 8, CHAN), ("row", "col"), 0, 0)
    block, partial, sent = call(
        second_kernel,
        [((TOK, MODEL), F32), ((TOK, MODEL), F32), ((1024, CHAN), BF)],
        [came.reshape(1024, CHAN), whole, row_packed, in_weight, out_turned],
        [tall, wide],
    )
    came = lax.all_to_all(sent.reshape(128, 8, CHAN), ("row", "col"), 0, 0)
    (sums,) = call(sum_kernel, [((128, 16, 128), BF)], [came])
    sums = lax.all_to_all(sums, ("row", "col"), 0, 0).reshape(2048, 128)
    pieces = call(
        return_kernel,
        [((64, CHAN), BF)] * 8,
        [place, came, partial, block],
        [((2, 1024, 128), F32), ((2, TOK, 128), F32), ((TOK, CHAN), BF)],
    )
    block, grad, in_grad, out_grad = call(
        last_kernel,
        [((TOK, MODEL), BF)] * 2 + [((MODEL, 2 * CHAN), F32), ((MODEL, CHAN), F32)],
        [place, sums, *swap_rows(pieces)],
        [((8, 3, 64, 128), F32), tall, ((2048, 128), F32)],
    )
    return (block.reshape(16, 32, MODEL), grad.reshape(16, 32, MODEL), in_grad, out_grad.T)


def solution(mesh):
    in_specs = (
        P("row", "col", None),
        P("row", "col", None, None),
        P("row", "col", None, None),
        P(),
        P(),
        P("row", "col", None),
    )
    out_specs = (P("row", "col", None), P("row", "col", None), P(), P())
    return jax.shard_map(
        on_device, mesh=mesh, in_specs=in_specs, out_specs=out_specs, check_vma=False
    )
```

```python
import jax
import jax.numpy as jnp
from jax import lax
from jax.experimental import pallas as pl
from jax.experimental.pallas import tpu as pltpu
from jax.sharding import PartitionSpec as P

BF = jnp.bfloat16
F32 = jnp.float32
MODEL = 192
CHAN = 384
TOK = 512
GROUP = 256
VMEM_LIMIT = 48 * 1024 * 1024


def iota(shape, dim):
    return lax.broadcasted_iota(jnp.int32, shape, dim)


def mm(a, b):
    return jnp.dot(a, b, preferred_element_type=F32)


def mm_t(a, b):
    return lax.dot_general(a, b, (((1,), (1,)), ((), ())), preferred_element_type=F32)


def t_mm(a, b):
    return lax.dot_general(a, b, (((0,), (0,)), ((), ())), preferred_element_type=F32)


def column_of(place):
    return (place % 8) * 32 + place // 8


HALVES = (slice(0, GROUP), slice(GROUP, TOK))


def prepare_scan(aux, by_row, forward):
    token = iota((TOK, 128), 0)
    chunk = (token // GROUP) * 4 + (token % 8) // 2 if by_row else token // 64
    member = (iota((TOK, 128), 1) // 16 == chunk).astype(F32)
    lane = iota((256, 640), 1)
    wanted = jnp.where(lane < 128, 192 + lane % 16, 208 + lane % 16)
    wanted = jnp.where(lane < 256, wanted, 220 + lane // 64)
    spread = mm(aux, (iota((256, 640), 0) == wanted).astype(F32).astype(BF))
    b_part = (spread[:, 0:128] * member).astype(BF)
    c_part = (spread[:, 128:256] * member).astype(BF)
    log_step = spread[:, 256:].astype(BF)
    here, there = iota((GROUP, GROUP), 0), iota((GROUP, GROUP), 1)
    if by_row:
        here, there = column_of(here), column_of(there)
    same = here // 64 == there // 64
    if forward:
        order, counted, src, out = there <= here, there <= here, b_part, c_part
    else:
        order, counted, src, out = there >= here, there > here, c_part, b_part
    add_up = (same & counted).astype(F32).astype(BF)
    run = jnp.concatenate([mm(add_up, log_step[h]) for h in HALVES], axis=0)
    decay = jnp.exp(t_mm(member.astype(BF), log_step))
    scores = [jnp.where(order, mm_t(out[h], src[h]), 0.0).astype(BF) for h in HALVES]
    return jnp.concatenate(scores, axis=0), src, out, jnp.exp(-run), jnp.exp(run), decay


def apply_scan(prepared, values, by_row, forward):
    scores, src, out, up, down, decay = prepared
    raised = (up[...] * values).astype(BF)
    states = t_mm(src[...], raised)
    zero = jnp.zeros((16, CHAN), F32)
    carried = [zero] * 8
    part = lambda array, k: array[16 * k : 16 * k + 16]
    if by_row:
        steps = [(k, k + 1) for k in range(7)] if forward else [(k, k - 1) for k in range(7, 0, -1)]
    else:
        steps = [(2 * j, 2 * j + 1) if forward else (2 * j + 1, 2 * j) for j in range(4)]
    for old, new in steps:
        carried[new] = part(decay, old) * (carried[old] + part(states, old))
    coming = jnp.concatenate(carried, axis=0).astype(BF)
    inner = jnp.concatenate([mm(scores[h, :], raised[h]) for h in HALVES], axis=0)
    return down[...] * (inner + mm(out[...], coming))


def scan_tokens(aux, values, by_row, forward):
    return apply_scan(prepare_scan(aux, by_row, forward), values, by_row, forward)


def lane_tile(l):
    return slice(128 * l, 128 * l + 128)


def row_places():
    for g in range(2):
        for r in range(8):
            for j in range(4):
                yield g * GROUP + (r * 4 + j) * 8, (r * 16 + g * 8) * 8 + j


def to_columns(scratch, value):
    for l in range(CHAN // 128):
        for place, row in row_places():
            scratch[l, pl.ds(row, 8, stride=8), :] = value[place : place + 8, lane_tile(l)]


def by_column(scratch, l):
    return jnp.concatenate([scratch[l, pl.ds(j, 128, stride=8), :] for j in range(4)], axis=0)


def split_lanes(ref, value):
    for l in range(value.shape[1] // 128):
        ref[l] = value[:, 128 * l : 128 * l + 128]


def peers(place, k):
    x, core = place[0] // 2, place[0] % 2
    return ((x + k // 2) % 4) * 2 + (core + k % 2) % 2


def with_aux(feat, sel, log, slot):
    index, lane = iota((48, 128), 0), iota((48, 128), 1)
    pick = ((lane == index + 64) & (index < 38)).astype(F32).astype(BF)
    blank = jnp.zeros((10, 32), F32)
    aux = []
    for i in range(16):
        chosen = sel[i, 32 * slot : 32 * slot + 32, :].astype(F32)
        decay = log[i].astype(F32)[:, slot, :]
        aux.append(t_mm(jnp.concatenate([chosen, decay, blank], axis=0).astype(BF), pick))
    upper = feat[:, 128:MODEL].astype(F32)
    upper = jnp.concatenate([upper, jnp.zeros((TOK, 64), F32)], axis=1)
    return (upper + jnp.concatenate(aux, axis=0)).astype(BF)


def pack_rows_kernel(feat, sel, log, packed):
    packed[:, 0:128] = feat[:, 0:128]
    packed[:, 128:256] = with_aux(feat, sel, log, 0)


def pack_columns_kernel(place, feat, cot, sel, log, *outs):
    slot = iota((TOK, 1), 0)
    row, j = slot % 16, (slot % 64) // 16
    dest = peers(place, slot // 64)
    choose = ((row * 32 + 4 * dest + j) == iota((TOK, TOK), 1)).astype(F32).astype(BF)
    left = mm(choose, feat[:, 0:128]).astype(BF)
    middle = mm(choose, with_aux(feat, sel, log, 1)).astype(BF)
    right = mm(choose, cot[...]).astype(BF)
    for k in range(4):
        rows = slice(128 * k, 128 * k + 128)
        outs[k][:, 0:128] = left[rows]
        outs[k][:, 128:256] = middle[rows]
        outs[k][:, 256 : 256 + MODEL] = right[rows]
        outs[k][:, 256 + MODEL :] = jnp.zeros((128, 64), BF)


def row_forward_kernel(packed, w_in, out, turned):
    move = (column_of(iota((GROUP, GROUP), 0)) == iota((GROUP, GROUP), 1)).astype(F32).astype(BF)
    for h in HALVES:
        turned[h, :] = mm(move, packed[h, :]).astype(BF)
    aux = turned[...]
    values = mm(aux[:, :MODEL], w_in[:, :CHAN]).astype(BF).astype(F32)
    out[...] = scan_tokens(aux, values, True, True).astype(BF)


def gate_terms(aux, cot, w_in, w_out):
    gate = mm(aux[:, :MODEL], w_in[:, CHAN:]).astype(BF).astype(F32)
    sig = 1.0 / (1.0 + jnp.exp(-gate))
    return gate, sig, mm(cot, w_out[...])


def sender(place, k):
    x, core = place[0] // 2, place[0] % 2
    return ((x + 4 - k // 2) % 4) * 2 + (core + k % 2) % 2


def col_adjoint_kernel(place, row_out, w_in, w_out, *refs):
    pieces, (out, whole, scratch) = refs[:8], refs[8:]
    for k in range(8):
        half, first = k % 2, 64 * (k % 2)
        source = sender(place, k)
        for j in range(4):
            rows = pl.ds(pl.multiple_of(128 * j + source * 16, 16), 16)
            whole[rows, :] = pieces[4 * half + k // 2][first + 16 * j : first + 16 * j + 16, :]
    aux = whole[:, :256]
    cot = whole[:, 256 : 256 + MODEL]
    gate, sig, hidden_grad = gate_terms(aux, cot, w_in, w_out)
    col_grad = (hidden_grad * gate * sig).astype(BF).astype(F32)
    row_grad = scan_tokens(aux, col_grad, False, False)
    to_columns(scratch, row_out[...].astype(F32))
    for l in range(3):
        for j in range(4):
            rows = slice(128 * j, 128 * j + 128)
            scratch[l, pl.ds(4 + j, 128, stride=8), :] = row_grad[rows, lane_tile(l)]
    for l in range(3):
        out[:, lane_tile(l)] = scratch[l].astype(BF)


def second_kernel(came, whole, packed, w_in, w_out, block, partial, out, scratch):
    split_lanes(scratch, came[...].astype(F32))
    row_out = jnp.concatenate([by_column(scratch, l) for l in range(3)], axis=1)
    row_grad = [
        jnp.concatenate(
            [scratch[l, pl.ds(row + 4, 8, stride=8), :] for _, row in row_places()], axis=0
        )
        for l in range(3)
    ]
    row_grad = jnp.concatenate(row_grad, axis=1)
    feat = whole[:, :MODEL]
    cot = whole[:, 256 : 256 + MODEL]
    col_out = scan_tokens(whole[:, :256], row_out, False, True).astype(BF).astype(F32)
    gate, sig, hidden_grad = gate_terms(feat, cot, w_in, w_out)
    hidden = (col_out * gate * sig).astype(BF)
    block[...] = feat.astype(F32) + mm_t(hidden, w_out[...])
    gate_grad = (hidden_grad * col_out * sig * (1.0 + gate * (1.0 - sig))).astype(BF)
    partial[...] = cot.astype(F32) + mm_t(gate_grad, w_in[:, CHAN:])
    shifted = jnp.concatenate([jnp.zeros((TOK, MODEL), F32), cot.astype(F32)], axis=1).astype(BF)
    out_part = t_mm(hidden, shifted)
    gate_part = t_mm(feat, gate_grad)

    value_grad = scan_tokens(packed[...], row_grad, True, False).astype(BF)
    pull = mm_t(value_grad, w_in[:, :CHAN])
    pull = jnp.concatenate([pull, jnp.zeros((TOK, MODEL), F32)], axis=1)
    value_part = t_mm(packed[:, :MODEL], value_grad)

    to_columns(scratch, pull)
    in_part = jnp.concatenate([value_part, gate_part], axis=0)
    for l in range(3):
        lanes = slice(128 * l, 128 * l + 128)
        for k in range(3):
            rows = slice(128 * k, 128 * k + 128)
            scratch[l, pl.ds(4 + k, 128, stride=8), :] = in_part[rows, lanes]
            if l > 0:
                scratch[l, pl.ds(k, 128, stride=8), :] += out_part[rows, lanes]
        scratch[l, pl.ds(7, 128, stride=8), :] = jnp.zeros((128, 128), F32)
    for l in range(3):
        out[:, 128 * l : 128 * l + 128] = scratch[l].astype(BF)


def sum_kernel(came, sums):
    total = jnp.sum(came[...].astype(F32), axis=0) * (65536.0**-0.5)
    tiles = [total[4 + k : 5 + k, 128 * l : 128 * l + 128] for k in range(3) for l in range(3)]
    tiles += [total[k : k + 1, 128 * l : 128 * l + 128] for k in range(3) for l in (1, 2)]
    tiles.append(jnp.zeros((1, 128), F32))
    slice_ = jnp.concatenate(tiles, axis=0).astype(BF)
    sums[...] = jnp.broadcast_to(slice_[None], (128, 16, 128))


def return_kernel(place, came, partial, block, *refs):
    outs, (scratch, whole) = refs[:8], refs[8:]
    for l in range(2):
        scratch[l] = came[:, :, 128 * l : 128 * l + 128].astype(F32).reshape(1024, 128)
    pull = jnp.concatenate([by_column(scratch, 0), by_column(scratch, 1)[:, :64]], axis=1)
    whole[...] = jnp.concatenate([block[...], partial[...] + pull], axis=1).astype(BF)
    for k in range(8):
        dest = peers(place, k)
        for j in range(4):
            rows = pl.ds(pl.multiple_of(128 * j + dest * 16, 16), 16)
            outs[k][16 * j : 16 * j + 16, :] = whole[rows, :]


def last_kernel(place, sums, *refs):
    pieces, (block, grad, in_grad, out_grad, whole, weights) = refs[:8], refs[8:]
    weights[...] = sums[...].astype(F32)
    strided = lambda first: weights[pl.ds(first, 128, stride=16), :]
    for l in range(3):
        lanes = slice(128 * l, 128 * l + 128)
        gate_lanes = slice(CHAN + 128 * l, CHAN + 128 * l + 128)
        in_grad[0:128, lanes] = strided(l)
        middle = strided(3 + l)
        in_grad[128:192, lanes] = middle[0:64]
        in_grad[0:64, gate_lanes] = middle[64:128]
        in_grad[64:192, gate_lanes] = strided(6 + l)
    for k in range(3):
        lanes = slice(128 * k, 128 * k + 128)
        out_grad[0:64, lanes] = strided(9 + 2 * k).T[64:128]
        out_grad[64:192, lanes] = strided(10 + 2 * k).T
    for k in range(8):
        first = 4 * sender(place, k)
        value = pieces[k][...].astype(F32)
        for l in range(3):
            for j in range(4):
                rows = slice(16 * j, 16 * j + 16)
                whole[l, pl.ds(first + j, 16, stride=32), :] = value[rows, lane_tile(l)]
    middle = whole[1]
    block[...] = jnp.concatenate([whole[0], middle[:, :64]], axis=1).astype(BF)
    grad[...] = jnp.concatenate([middle[:, 64:], whole[2]], axis=1).astype(BF)


def call(kernel, outs, ins, scratch=(), flops=10**8, vmem=VMEM_LIMIT):
    specs = [pl.BlockSpec()] * len(ins)
    if ins[0].shape == (1,):
        specs[0] = pl.BlockSpec(memory_space=pltpu.SMEM)
    return pl.pallas_call(
        kernel,
        out_shape=[jax.ShapeDtypeStruct(shape, dtype) for shape, dtype in outs],
        in_specs=specs,
        out_specs=[pl.BlockSpec()] * len(outs),
        scratch_shapes=[pltpu.VMEM(shape, dtype) for shape, dtype in scratch],
        compiler_params=pltpu.CompilerParams(vmem_limit_bytes=vmem),
        cost_estimate=pl.CostEstimate(flops=flops, bytes_accessed=10**6, transcendentals=10**5),
    )(*ins)


def swap_rows(pieces):
    pairs = lambda k: [(i, ((i // 2 + k // 2) % 4) * 2 + (i + k) % 2) for i in range(8)]
    return [pieces[0]] + [lax.ppermute(pieces[k], "row", pairs(k)) for k in range(1, 8)]


def swap_rows_in_steps(pieces):
    along = lambda s: [(i, (i + 2 * s) % 8) for i in range(8)]
    mine = [pieces[0]] + [lax.ppermute(pieces[s], "row", along(s)) for s in (1, 2, 3)]
    return mine + [lax.ppermute(piece, "row", [(i, i ^ 1) for i in range(8)]) for piece in mine]


def on_device(features, selectors, log_decay, in_weight, out_weight, cotangent):
    place = lax.axis_index("row").astype(jnp.int32).reshape(1)
    out_turned = out_weight.T
    feat = features.reshape(TOK, MODEL)
    sel = selectors.transpose(0, 2, 3, 1).reshape(16, 64, 32)
    log = log_decay.transpose(0, 3, 2, 1)
    wide = ((3, 1024, 128), F32)
    (row_packed,) = call(
        pack_rows_kernel, [((TOK, 256), BF)], [feat, sel, log], vmem=60 * 1024 * 1024
    )
    row_packed = lax.all_to_all(row_packed.reshape(16, 32, 256), "col", 0, 0).reshape(TOK, 256)
    pieces = call(
        pack_columns_kernel,
        [((128, 512), BF)] * 4,
        [place, feat, cotangent.reshape(TOK, MODEL), sel, log],
    )
    pieces = swap_rows_in_steps(pieces)
    row_out, row_packed = call(
        row_forward_kernel,
        [((TOK, CHAN), BF), ((TOK, 256), BF)],
        [row_packed, in_weight],
        flops=3 * 10**10,
    )
    sent, whole = call(
        col_adjoint_kernel,
        [((1024, CHAN), BF), ((TOK, 512), BF)],
        [place, row_out, in_weight, out_turned, *pieces],
        [wide],
    )
    came = lax.all_to_all(sent.reshape(128, 8, CHAN), ("row", "col"), 0, 0)
    block, partial, sent = call(
        second_kernel,
        [((TOK, MODEL), F32), ((TOK, MODEL), F32), ((1024, CHAN), BF)],
        [came.reshape(1024, CHAN), whole, row_packed, in_weight, out_turned],
        [wide],
    )
    came = lax.all_to_all(sent.reshape(128, 8, CHAN), ("row", "col"), 0, 0)
    (sums,) = call(sum_kernel, [((128, 16, 128), BF)], [came])
    sums = lax.all_to_all(sums, ("row", "col"), 0, 0).reshape(2048, 128)
    pieces = call(
        return_kernel,
        [((64, CHAN), BF)] * 8,
        [place, came, partial, block],
        [((2, 1024, 128), F32), ((TOK, CHAN), BF)],
    )
    block, grad, in_grad, out_grad = call(
        last_kernel,
        [((TOK, MODEL), BF)] * 2 + [((MODEL, 2 * CHAN), F32), ((MODEL, CHAN), F32)],
        [place, sums, *swap_rows(pieces)],
        [((3, TOK, 128), F32), ((2048, 128), F32)],
    )
    return (block.reshape(16, 32, MODEL), grad.reshape(16, 32, MODEL), in_grad, out_grad.T)


def solution(mesh):
    in_specs = (
        P("row", "col", None),
        P("row", "col", None, None),
        P("row", "col", None, None),
        P(),
        P(),
        P("row", "col", None),
    )
    out_specs = (P("row", "col", None), P("row", "col", None), P(), P())
    return jax.shard_map(
        on_device, mesh=mesh, in_specs=in_specs, out_specs=out_specs, check_vma=False
    )
```

```python
import jax
import jax.numpy as jnp
from jax import lax
from jax.experimental import pallas as pl
from jax.experimental.pallas import tpu as pltpu
from jax.sharding import PartitionSpec as P

BF = jnp.bfloat16
F32 = jnp.float32
MODEL = 192
CHAN = 384
TOK = 512
GROUP = 256
VMEM_LIMIT = 48 * 1024 * 1024


def iota(shape, dim):
    return lax.broadcasted_iota(jnp.int32, shape, dim)


def mm(a, b):
    return jnp.dot(a, b, preferred_element_type=F32)


def mm_t(a, b):
    return lax.dot_general(a, b, (((1,), (1,)), ((), ())), preferred_element_type=F32)


def t_mm(a, b):
    return lax.dot_general(a, b, (((0,), (0,)), ((), ())), preferred_element_type=F32)


def column_of(place):
    return (place % 8) * 32 + place // 8


HALVES = (slice(0, GROUP), slice(GROUP, TOK))


def prepare_scan(aux, by_row, forward):
    token = iota((TOK, 128), 0)
    chunk = (token // GROUP) * 4 + (token % 8) // 2 if by_row else token // 64
    member = (iota((TOK, 128), 1) // 16 == chunk).astype(F32)
    lane = iota((256, 640), 1)
    wanted = jnp.where(lane < 128, 192 + lane % 16, 208 + lane % 16)
    wanted = jnp.where(lane < 256, wanted, 220 + lane // 64)
    spread = mm(aux, (iota((256, 640), 0) == wanted).astype(F32).astype(BF))
    b_part = (spread[:, 0:128] * member).astype(BF)
    c_part = (spread[:, 128:256] * member).astype(BF)
    log_step = spread[:, 256:].astype(BF)
    here, there = iota((GROUP, GROUP), 0), iota((GROUP, GROUP), 1)
    if by_row:
        here, there = column_of(here), column_of(there)
    same = here // 64 == there // 64
    if forward:
        order, counted, src, out = there <= here, there <= here, b_part, c_part
    else:
        order, counted, src, out = there >= here, there > here, c_part, b_part
    add_up = (same & counted).astype(F32).astype(BF)
    run = jnp.concatenate([mm(add_up, log_step[h]) for h in HALVES], axis=0)
    decay = jnp.exp(t_mm(member.astype(BF), log_step))
    scores = [jnp.where(order, mm_t(out[h], src[h]), 0.0).astype(BF) for h in HALVES]
    return jnp.concatenate(scores, axis=0), src, out, jnp.exp(-run), jnp.exp(run), decay


def apply_scan(prepared, values, by_row, forward):
    scores, src, out, up, down, decay = prepared
    raised = (up[...] * values).astype(BF)
    states = t_mm(src[...], raised)
    zero = jnp.zeros((16, CHAN), F32)
    carried = [zero] * 8
    part = lambda array, k: array[16 * k : 16 * k + 16]
    if by_row:
        steps = [(k, k + 1) for k in range(7)] if forward else [(k, k - 1) for k in range(7, 0, -1)]
    else:
        steps = [(2 * j, 2 * j + 1) if forward else (2 * j + 1, 2 * j) for j in range(4)]
    for old, new in steps:
        carried[new] = part(decay, old) * (carried[old] + part(states, old))
    coming = jnp.concatenate(carried, axis=0).astype(BF)
    inner = jnp.concatenate([mm(scores[h, :], raised[h]) for h in HALVES], axis=0)
    return down[...] * (inner + mm(out[...], coming))


def scan_tokens(aux, values, by_row, forward):
    return apply_scan(prepare_scan(aux, by_row, forward), values, by_row, forward)


def lane_tile(l):
    return slice(128 * l, 128 * l + 128)


def row_places():
    for g in range(2):
        for r in range(8):
            for j in range(4):
                yield g * GROUP + (r * 4 + j) * 8, (r * 16 + g * 8) * 8 + j


def to_columns(scratch, value):
    for l in range(CHAN // 128):
        for place, row in row_places():
            scratch[l, pl.ds(row, 8, stride=8), :] = value[place : place + 8, lane_tile(l)]


def by_column(scratch, l):
    return jnp.concatenate([scratch[l, pl.ds(j, 128, stride=8), :] for j in range(4)], axis=0)


def split_lanes(ref, value):
    for l in range(value.shape[1] // 128):
        ref[l] = value[:, 128 * l : 128 * l + 128]


def peers(place, k):
    x, core = place[0] // 2, place[0] % 2
    return ((x + k // 2) % 4) * 2 + (core + k % 2) % 2


def with_aux(feat, sel, log, slot):
    index, lane = iota((48, 128), 0), iota((48, 128), 1)
    pick = ((lane == index + 64) & (index < 38)).astype(F32).astype(BF)
    blank = jnp.zeros((10, 32), F32)
    aux = []
    for i in range(16):
        chosen = sel[i, 32 * slot : 32 * slot + 32, :].astype(F32)
        decay = log[i].astype(F32)[:, slot, :]
        aux.append(t_mm(jnp.concatenate([chosen, decay, blank], axis=0).astype(BF), pick))
    upper = feat[:, 128:MODEL].astype(F32)
    upper = jnp.concatenate([upper, jnp.zeros((TOK, 64), F32)], axis=1)
    return (upper + jnp.concatenate(aux, axis=0)).astype(BF)


def pack_rows_kernel(feat, sel, log, packed):
    packed[:, 0:128] = feat[:, 0:128]
    packed[:, 128:256] = with_aux(feat, sel, log, 0)


def pack_columns_kernel(place, feat, cot, sel, log, *outs):
    slot = iota((TOK, 1), 0)
    row, j = slot % 16, (slot % 64) // 16
    dest = peers(place, slot // 64)
    choose = ((row * 32 + 4 * dest + j) == iota((TOK, TOK), 1)).astype(F32).astype(BF)
    left = mm(choose, feat[:, 0:128]).astype(BF)
    middle = mm(choose, with_aux(feat, sel, log, 1)).astype(BF)
    right = mm(choose, cot[...]).astype(BF)
    for k in range(4):
        rows = slice(128 * k, 128 * k + 128)
        outs[k][:, 0:128] = left[rows]
        outs[k][:, 128:256] = middle[rows]
        outs[k][:, 256 : 256 + MODEL] = right[rows]
        outs[k][:, 256 + MODEL :] = jnp.zeros((128, 64), BF)


def row_forward_kernel(packed, w_in, out, turned):
    move = (column_of(iota((GROUP, GROUP), 0)) == iota((GROUP, GROUP), 1)).astype(F32).astype(BF)
    for h in HALVES:
        turned[h, :] = mm(move, packed[h, :]).astype(BF)
    aux = turned[...]
    values = mm(aux[:, :MODEL], w_in[:, :CHAN]).astype(BF).astype(F32)
    out[...] = scan_tokens(aux, values, True, True).astype(BF)


def gate_terms(aux, cot, w_in, w_out):
    gate = mm(aux[:, :MODEL], w_in[:, CHAN:]).astype(BF).astype(F32)
    sig = 1.0 / (1.0 + jnp.exp(-gate))
    return gate, sig, mm(cot, w_out[...])


def sender(place, k):
    x, core = place[0] // 2, place[0] % 2
    return ((x + 4 - k // 2) % 4) * 2 + (core + k % 2) % 2


def col_adjoint_kernel(place, row_out, w_in, w_out, *refs):
    pieces, (out, whole, scratch) = refs[:8], refs[8:]
    for k in range(8):
        half, first = k % 2, 64 * (k % 2)
        source = sender(place, k)
        for j in range(4):
            rows = pl.ds(pl.multiple_of(128 * j + source * 16, 16), 16)
            whole[rows, :] = pieces[4 * half + k // 2][first + 16 * j : first + 16 * j + 16, :]
    aux = whole[:, :256]
    cot = whole[:, 256 : 256 + MODEL]
    gate, sig, hidden_grad = gate_terms(aux, cot, w_in, w_out)
    col_grad = (hidden_grad * gate * sig).astype(BF).astype(F32)
    row_grad = scan_tokens(aux, col_grad, False, False)
    to_columns(scratch, row_out[...].astype(F32))
    for l in range(3):
        for j in range(4):
            rows = slice(128 * j, 128 * j + 128)
            scratch[l, pl.ds(4 + j, 128, stride=8), :] = row_grad[rows, lane_tile(l)]
    for l in range(3):
        out[:, lane_tile(l)] = scratch[l].astype(BF)


def second_kernel(came, whole, packed, w_in, w_out, block, partial, out, scratch):
    split_lanes(scratch, came[...].astype(F32))
    row_out = jnp.concatenate([by_column(scratch, l) for l in range(3)], axis=1)
    row_grad = [
        jnp.concatenate(
            [scratch[l, pl.ds(row + 4, 8, stride=8), :] for _, row in row_places()], axis=0
        )
        for l in range(3)
    ]
    row_grad = jnp.concatenate(row_grad, axis=1)
    feat = whole[:, :MODEL]
    cot = whole[:, 256 : 256 + MODEL]
    col_out = scan_tokens(whole[:, :256], row_out, False, True).astype(BF).astype(F32)
    gate, sig, hidden_grad = gate_terms(feat, cot, w_in, w_out)
    hidden = (col_out * gate * sig).astype(BF)
    block[...] = feat.astype(F32) + mm_t(hidden, w_out[...])
    gate_grad = (hidden_grad * col_out * sig * (1.0 + gate * (1.0 - sig))).astype(BF)
    partial[...] = cot.astype(F32) + mm_t(gate_grad, w_in[:, CHAN:])
    shifted = jnp.concatenate([jnp.zeros((TOK, MODEL), F32), cot.astype(F32)], axis=1).astype(BF)
    out_part = t_mm(hidden, shifted)
    gate_part = t_mm(feat, gate_grad)

    value_grad = scan_tokens(packed[...], row_grad, True, False).astype(BF)
    pull = mm_t(value_grad, w_in[:, :CHAN])
    pull = jnp.concatenate([pull, jnp.zeros((TOK, MODEL), F32)], axis=1)
    value_part = t_mm(packed[:, :MODEL], value_grad)

    to_columns(scratch, pull)
    in_part = jnp.concatenate([value_part, gate_part], axis=0)
    for l in range(3):
        lanes = slice(128 * l, 128 * l + 128)
        for k in range(3):
            rows = slice(128 * k, 128 * k + 128)
            scratch[l, pl.ds(4 + k, 128, stride=8), :] = in_part[rows, lanes]
            if l > 0:
                scratch[l, pl.ds(k, 128, stride=8), :] += out_part[rows, lanes]
        scratch[l, pl.ds(7, 128, stride=8), :] = jnp.zeros((128, 128), F32)
    for l in range(3):
        out[:, 128 * l : 128 * l + 128] = scratch[l].astype(BF)


def sum_kernel(came, sums):
    total = jnp.sum(came[...].astype(F32), axis=0) * (65536.0**-0.5)
    tiles = [total[4 + k : 5 + k, 128 * l : 128 * l + 128] for k in range(3) for l in range(3)]
    tiles += [total[k : k + 1, 128 * l : 128 * l + 128] for k in range(3) for l in (1, 2)]
    tiles.append(jnp.zeros((1, 128), F32))
    slice_ = jnp.concatenate(tiles, axis=0).astype(BF)
    sums[...] = jnp.broadcast_to(slice_[None], (128, 16, 128))


def return_kernel(place, came, partial, block, *refs):
    outs, (scratch, whole) = refs[:8], refs[8:]
    for l in range(2):
        scratch[l] = came[:, :, 128 * l : 128 * l + 128].astype(F32).reshape(1024, 128)
    pull = jnp.concatenate([by_column(scratch, 0), by_column(scratch, 1)[:, :64]], axis=1)
    whole[...] = jnp.concatenate([block[...], partial[...] + pull], axis=1).astype(BF)
    for k in range(8):
        dest = peers(place, k)
        for j in range(4):
            rows = pl.ds(pl.multiple_of(128 * j + dest * 16, 16), 16)
            outs[k][16 * j : 16 * j + 16, :] = whole[rows, :]


SENT = (0, 4, 5, 2, 3, 6, 7, 1)


def last_kernel(place, sums, *refs):
    pieces, (block, grad, in_grad, out_grad, whole, weights) = refs[:8], refs[8:]
    weights[...] = sums[...].astype(F32)
    strided = lambda first: weights[pl.ds(first, 128, stride=16), :]
    for l in range(3):
        lanes = slice(128 * l, 128 * l + 128)
        gate_lanes = slice(CHAN + 128 * l, CHAN + 128 * l + 128)
        in_grad[0:128, lanes] = strided(l)
        middle = strided(3 + l)
        in_grad[128:192, lanes] = middle[0:64]
        in_grad[0:64, gate_lanes] = middle[64:128]
        in_grad[64:192, gate_lanes] = strided(6 + l)
    for k in range(3):
        lanes = slice(128 * k, 128 * k + 128)
        out_grad[0:64, lanes] = strided(9 + 2 * k).T[64:128]
        out_grad[64:192, lanes] = strided(10 + 2 * k).T
    for k in range(8):
        first = 4 * sender(place, k)
        value = pieces[SENT.index(k)][...].astype(F32)
        for l in range(3):
            for j in range(4):
                rows = slice(16 * j, 16 * j + 16)
                whole[l, pl.ds(first + j, 16, stride=32), :] = value[rows, lane_tile(l)]
    middle = whole[1]
    block[...] = jnp.concatenate([whole[0], middle[:, :64]], axis=1).astype(BF)
    grad[...] = jnp.concatenate([middle[:, 64:], whole[2]], axis=1).astype(BF)


def call(kernel, outs, ins, scratch=(), flops=10**8, vmem=VMEM_LIMIT):
    specs = [pl.BlockSpec()] * len(ins)
    if ins[0].shape == (1,):
        specs[0] = pl.BlockSpec(memory_space=pltpu.SMEM)
    return pl.pallas_call(
        kernel,
        out_shape=[jax.ShapeDtypeStruct(shape, dtype) for shape, dtype in outs],
        in_specs=specs,
        out_specs=[pl.BlockSpec()] * len(outs),
        scratch_shapes=[pltpu.VMEM(shape, dtype) for shape, dtype in scratch],
        compiler_params=pltpu.CompilerParams(vmem_limit_bytes=vmem),
        cost_estimate=pl.CostEstimate(flops=flops, bytes_accessed=10**6, transcendentals=10**5),
    )(*ins)


def swap_rows(pieces):
    pairs = lambda k: [(i, ((i // 2 + k // 2) % 4) * 2 + (i + k) % 2) for i in range(8)]
    came = {0: pieces[0]}
    for k in SENT[1:]:
        came[k] = lax.ppermute(pieces[k], "row", pairs(k))
    return [came[k] for k in SENT]


def swap_rows_in_steps(pieces):
    along = lambda s: [(i, (i + 2 * s) % 8) for i in range(8)]
    mine = [pieces[0]] + [lax.ppermute(pieces[s], "row", along(s)) for s in (1, 2, 3)]
    return mine + [lax.ppermute(piece, "row", [(i, i ^ 1) for i in range(8)]) for piece in mine]


def on_device(features, selectors, log_decay, in_weight, out_weight, cotangent):
    place = lax.axis_index("row").astype(jnp.int32).reshape(1)
    out_turned = out_weight.T
    feat = features.reshape(TOK, MODEL)
    sel = selectors.transpose(0, 2, 3, 1).reshape(16, 64, 32)
    log = log_decay.transpose(0, 3, 2, 1)
    wide = ((3, 1024, 128), F32)
    (row_packed,) = call(
        pack_rows_kernel, [((TOK, 256), BF)], [feat, sel, log], vmem=60 * 1024 * 1024
    )
    row_packed = lax.all_to_all(row_packed.reshape(16, 32, 256), "col", 0, 0).reshape(TOK, 256)
    pieces = call(
        pack_columns_kernel,
        [((128, 512), BF)] * 4,
        [place, feat, cotangent.reshape(TOK, MODEL), sel, log],
    )
    pieces = swap_rows_in_steps(pieces)
    row_out, row_packed = call(
        row_forward_kernel,
        [((TOK, CHAN), BF), ((TOK, 256), BF)],
        [row_packed, in_weight],
        flops=3 * 10**10,
    )
    sent, whole = call(
        col_adjoint_kernel,
        [((1024, CHAN), BF), ((TOK, 512), BF)],
        [place, row_out, in_weight, out_turned, *pieces],
        [wide],
    )
    came = lax.all_to_all(sent.reshape(128, 8, CHAN), ("row", "col"), 0, 0)
    block, partial, sent = call(
        second_kernel,
        [((TOK, MODEL), F32), ((TOK, MODEL), F32), ((1024, CHAN), BF)],
        [came.reshape(1024, CHAN), whole, row_packed, in_weight, out_turned],
        [wide],
    )
    came = lax.all_to_all(sent.reshape(128, 8, CHAN), ("row", "col"), 0, 0)
    (sums,) = call(sum_kernel, [((128, 16, 128), BF)], [came])
    sums = lax.all_to_all(sums, ("row", "col"), 0, 0).reshape(2048, 128)
    pieces = call(
        return_kernel,
        [((64, CHAN), BF)] * 8,
        [place, came, partial, block],
        [((2, 1024, 128), F32), ((TOK, CHAN), BF)],
    )
    block, grad, in_grad, out_grad = call(
        last_kernel,
        [((TOK, MODEL), BF)] * 2 + [((MODEL, 2 * CHAN), F32), ((MODEL, CHAN), F32)],
        [place, sums, *swap_rows(pieces)],
        [((3, TOK, 128), F32), ((2048, 128), F32)],
    )
    return (block.reshape(16, 32, MODEL), grad.reshape(16, 32, MODEL), in_grad, out_grad.T)


def solution(mesh):
    in_specs = (
        P("row", "col", None),
        P("row", "col", None, None),
        P("row", "col", None, None),
        P(),
        P(),
        P("row", "col", None),
    )
    out_specs = (P("row", "col", None), P("row", "col", None), P(), P())
    return jax.shard_map(
        on_device, mesh=mesh, in_specs=in_specs, out_specs=out_specs, check_vma=False
    )
```
